32 devices in a mesh: rows: 8 (over z, y), feat: 4 (over x, core).
Axes of the slice: x: 2, y: 2, z: 4, core: 2. Of those that a mesh axis runs over, the one named last changes fastest.
Arguments:
- features: bfloat16 [32768, 128], P('rows', 'feat'), may hold values from -8 to 8
- lengths: int32 [8, 6], P('rows'), may hold values from 102 to 3586, as said below
- train_counts: int32 [8, 6], P('rows'), may hold values from 51 to 3585, as said below
- used_features: int32 [8, 6], P('rows'), may hold values from 50 to 100
- w_enc: bfloat16 [128, 512], P('feat'), may hold values from -0.625 to 0.625
- b_enc: float32 [512], replicated, may hold values from -3 to 3
- w_qkv: bfloat16 [512, 1536], replicated, may hold values from -0.25 to 0.25
- b_query: float32 [512], replicated, may hold values from -3 to 3
- b_value: float32 [512], replicated, may hold values from -3 to 3
- w_out: bfloat16 [512, 512], replicated, may hold values from -2 to 2
- b_out: float32 [512], replicated, may hold values from -2 to 2
- gain_one: float32 [512], replicated, may hold values from 0.5 to 1.5
- shift_one: float32 [512], replicated, may hold values from -2 to 2
- w_up: bfloat16 [512, 1024], replicated, may hold values from -0.25 to 0.25
- b_up: float32 [1024], replicated, may hold values from -3 to 3
- w_down: bfloat16 [1024, 512], replicated, may hold values from -0.25 to 0.25
- b_down: float32 [512], replicated, may hold values from -2 to 2
- gain_two: float32 [512], replicated, may hold values from 0.5 to 1.5
- shift_two: float32 [512], replicated, may hold values from -2 to 2
- cotangent: bfloat16 [32768, 512], P(('rows', 'feat')), may hold values from -6 to 6
Outputs:
- output: bfloat16 [32768, 512], P(('rows', 'feat'))
- grad_features: float32 [32768, 128], P('rows', 'feat')
- grad_w_enc: float32 [128, 512], P('feat')
- grad_b_enc: float32 [512], replicated
- grad_w_qkv: float32 [512, 1536], replicated
- grad_b_query: float32 [512], replicated
- grad_b_value: float32 [512], replicated
- grad_w_out: float32 [512, 512], replicated
- grad_b_out: float32 [512], replicated
- grad_gain_one: float32 [512], replicated
- grad_shift_one: float32 [512], replicated
- grad_w_up: float32 [512, 1024], replicated
- grad_b_up: float32 [1024], replicated
- grad_w_down: float32 [1024, 512], replicated
- grad_b_down: float32 [512], replicated
- grad_gain_two: float32 [512], replicated
- grad_shift_two: float32 [512], replicated
The draws below stay inside these ranges and needn't reach their ends.
Inputs may be any that keep to these rules, and one draw needn't show every extreme that they name: The lengths of a group sum to 4096; in each group one table, at a place drawn from the seed, holds more than half of the group's rows. `train_counts`: each table has at least lengths // 2 and fewer than all of its rows as train rows.
All inputs are finite; a program needn't handle non-finite values.
Results may differ from the reference program's by a relative error of at most 0.015.
Values may be sent and summed in bfloat16 or wider, within the bound.
A program may use at most 256 MiB of HBM per device.

```python
import math
import jax
import jax.numpy as jnp
from jax import lax

E = 512
HEADS = 4
HD = 128
FF = 1024
F = 128
FEATS = 100
TOK_GRP = 4096
TABS = 6
GROUPS = 8
TOKENS = 32768
N_FEAT = 4


def table_lengths(key):
    quarter = TOK_GRP // N_FEAT
    lowest = quarter // (2 * (TABS - 1))
    highest = quarter // (TABS - 1)
    key_small, key_place, key_group = jax.random.split(jax.random.fold_in(key, 11), 3)
    small = jax.random.randint(key_small, (GROUPS, TABS), lowest, highest + 1)
    chosen_group = jax.random.randint(key_group, (), 0, GROUPS)
    is_chosen = (jnp.arange(GROUPS, dtype=jnp.int32) == chosen_group)[:, None]
    small = jnp.where(is_chosen, lowest, small)
    placed = jax.random.randint(key_place, (GROUPS, 1), 0, TABS)
    is_big = jnp.arange(TABS, dtype=jnp.int32)[None, :] == placed
    small = jnp.where(is_big, 0, small)
    biggest = TOK_GRP - jnp.sum(small, axis=1, keepdims=True)
    table_len = jnp.where(is_big, biggest, small).astype(jnp.int32)
    return (table_len, is_chosen, is_big)


def draw_lengths(key, part):
    table_len, is_chosen, is_big = table_lengths(key)
    return table_len


def draw_train_counts(key, part):
    table_len, is_chosen, is_big = table_lengths(key)
    key = jax.random.fold_in(key, 5)
    drawn = jax.random.randint(key, table_len.shape, table_len // 2, table_len)
    fixed = jnp.where(is_big, table_len - 1, table_len // 2)
    return jnp.where(is_chosen, fixed, drawn).astype(jnp.int32)


def draw_features(key, part):
    key = jax.random.fold_in(key, 7)
    key_col, key_val = jax.random.split(key, 2)
    col_scale = jnp.exp(jax.random.uniform(key_col, (GROUPS, 1, F), jnp.float32, math.log(0.2), math.log(2.0)))
    values = jnp.clip(jax.random.normal(key_val, (GROUPS, TOK_GRP, F), jnp.float32), -4.0, 4.0)
    return jnp.clip(values * col_scale, -8.0, 8.0).reshape(TOKENS, F).astype(jnp.bfloat16)


def with_ends(values, own_key, least, high):
    dims = values.shape
    index_at = [jax.random.randint(jax.random.fold_in(own_key, axis), (), 0, dims[axis]) for axis in range(len(dims))]
    values = values.at[tuple(index_at)].set(least)
    longest = dims.index(max(dims))
    index_at[longest] = (index_at[longest] + 1) % dims[longest]
    return values.at[tuple(index_at)].set(high)


def block_levels(key, shape, cuts, low, largest):
    def one(position, shards_of):
        steps = jax.random.uniform(jax.random.fold_in(jax.random.fold_in(key, 6), position), (shards_of,), jnp.float32, low / len(cuts), largest / len(cuts))
        return jnp.repeat(jnp.exp(steps), shape[position] // shards_of).reshape((-1,) + (1,) * (len(shape) - position - 1))

    loudness = one(*cuts[0])
    for cut in cuts[1:]:
        loudness = loudness * one(*cut)
    return loudness


def scatter_about(key, shape, scale, reach, shards=(), kind=jnp.bfloat16):
    entries = jax.random.normal(key, shape, jnp.float32) * scale
    if len(shards) > 0:
        entries = block_levels(key, shape, shards, -0.22, 0.18) * entries
    return jnp.clip(entries, min=-reach, max=reach).astype(kind)


def setup_inputs(seed: int = 0) -> dict:
    seeds = jax.random.split(jax.random.key(seed), 21)
    return {
        "features": draw_features(jax.random.fold_in(seeds[20], 71), 0),
        "lengths": draw_lengths(jax.random.fold_in(seeds[20], 71), 0),
        "train_counts": draw_train_counts(jax.random.fold_in(seeds[20], 71), 0),
        "used_features": with_ends(jax.random.randint(seeds[3], (GROUPS, TABS), FEATS // 2, FEATS + 1), jax.random.fold_in(seeds[3], 1), FEATS // 2, FEATS).astype(jnp.int32),
        "w_enc": scatter_about(seeds[4], (F, E), FEATS ** -0.5, 0.625, ((0, 4),)),
        "b_enc": scatter_about(seeds[5], (E,), 0.5, 3.0, (), jnp.float32),
        "w_qkv": scatter_about(seeds[6], (E, 3 * E), E ** -0.5, 0.25),
        "b_query": scatter_about(seeds[7], (E,), 0.5, 3.0, (), jnp.float32),
        "b_value": scatter_about(seeds[8], (E,), 0.5, 3.0, (), jnp.float32),
        "w_out": scatter_about(seeds[9], (E, E), (max(8, E * 8 // TOK_GRP)) ** -0.5, 2.0),
        "b_out": scatter_about(seeds[10], (E,), 0.3, 2.0, (), jnp.float32),
        "gain_one": jnp.clip(1.0 + 0.1 * jax.random.normal(seeds[11], (E,), jnp.float32), 0.5, 1.5),
        "shift_one": scatter_about(seeds[12], (E,), 0.3, 2.0, (), jnp.float32),
        "w_up": scatter_about(seeds[13], (E, FF), E ** -0.5, 0.25),
        "b_up": scatter_about(seeds[14], (FF,), 0.5, 3.0, (), jnp.float32),
        "w_down": scatter_about(seeds[15], (FF, E), (FF // 2) ** -0.5, 0.25),
        "b_down": scatter_about(seeds[16], (E,), 0.3, 2.0, (), jnp.float32),
        "gain_two": jnp.clip(1.0 + 0.1 * jax.random.normal(seeds[17], (E,), jnp.float32), 0.5, 1.5),
        "shift_two": scatter_about(seeds[18], (E,), 0.3, 2.0, (), jnp.float32),
        "cotangent": scatter_about(seeds[19], (TOKENS, E), 1.0, 6.0, ((0, 32),)),
    }


HIGH = lax.Precision.HIGHEST

@jax.custom_vjp
def low(v):
    return lax.optimization_barrier(v.astype(jnp.bfloat16)).astype(jnp.float32)

@jax.custom_vjp
def low_back(v):
    return v

def low_keep(v):
    return (low(v), None)

def low_pass(kept, grad):
    return (grad,)

def back_keep(v):
    return (v, None)

def back_low(kept, grad):
    return (low(grad),)
low.defvjp(low_keep, low_pass)
low_back.defvjp(back_keep, back_low)

def layout(table_len, train_count, group_rows):
    tokens_at = jnp.arange(group_rows, dtype=jnp.int32)
    table_end = jnp.cumsum(table_len).astype(jnp.int32)
    starts = table_end - table_len
    inside = (tokens_at[:, None] >= starts[None, :]) & (tokens_at[:, None] < table_end[None, :])
    member = inside.astype(jnp.float32)
    learned = inside & (tokens_at[:, None] < (starts + train_count)[None, :])
    is_train = lax.optimization_barrier(jnp.sum(learned.astype(jnp.float32), axis=1))
    table_of = lax.optimization_barrier(jnp.sum((tokens_at[:, None] >= table_end[None, :]).astype(jnp.int32), axis=1))
    return (member, is_train, table_of)

def normalized(values, member, is_train, train_count, used_count, feature_col):
    train_rows = train_count.astype(jnp.float32)[:, None]
    col_mean = jnp.einsum('tg,tf->gf', member, values * is_train[:, None], precision=HIGH) / train_rows
    centred = values - jnp.dot(member, col_mean, precision=HIGH)
    col_var = jnp.einsum('tg,tf->gf', member, centred * centred * is_train[:, None], precision=HIGH) / train_rows
    keeper = (feature_col[None, :] < used_count[:, None]).astype(jnp.float32)
    factor = lax.rsqrt(jnp.maximum(col_var, 0.25)) * jnp.sqrt(FEATS / used_count.astype(jnp.float32))[:, None] * keeper
    return centred * jnp.dot(member, factor, precision=HIGH)

def layer_norm(values, gain, shift):
    centre = values - lax.optimization_barrier(jnp.mean(values, axis=1, keepdims=True))
    spread = lax.optimization_barrier(jnp.mean(centre * centre, axis=1, keepdims=True))
    return centre * lax.rsqrt(spread + 1e-05) * gain + shift

def forward(values, params, member, is_train, table_of, train_count, used_count):
    w_enc, b_enc, w_qkv, b_query, b_value, w_out, b_out, gain_one, shift_one, w_up, b_up, w_down, b_down, gain_two, shift_two = params
    group_rows = values.shape[0]
    width = w_qkv.shape[0]
    feature_col = jnp.arange(values.shape[1], dtype=jnp.int32)
    normed = low(normalized(values, member, is_train, train_count, used_count, feature_col))
    encoded = low_back(jnp.dot(normed, w_enc, precision=HIGH) + b_enc)
    projected = jnp.dot(low(encoded), w_qkv, precision=HIGH)
    query = low(low_back(projected[:, :width] + b_query))
    keys = low(low_back(projected[:, width:2 * width]))
    vals = low(low_back(projected[:, 2 * width:] + b_value))
    block_rows = min(512, group_rows)
    block_count = group_rows // block_rows
    inv_root = 1.0 / math.sqrt(HD)

    def one_block(args):
        query_blk, table_blk = args
        allowed = (table_blk[:, None] == table_of[None, :]) & (is_train[None, :] > 0.5)
        pieces = []
        for which_head in range(HEADS):
            lower = which_head * HD
            upper = lower + HD
            scores = low_back(jnp.dot(query_blk[:, lower:upper], keys[:, lower:upper].T, precision=HIGH) * inv_root)
            scores = jnp.where(allowed, scores, -1e+30)
            peak = lax.optimization_barrier(jnp.max(scores, axis=1, keepdims=True))
            weights = jnp.exp(scores - peak)
            probs = weights / lax.optimization_barrier(jnp.sum(weights, axis=1, keepdims=True))
            pieces.append(jnp.dot(low(probs), vals[:, lower:upper], precision=HIGH))
        return jnp.concatenate(pieces, axis=1)
    attended = lax.map(jax.checkpoint(one_block), (query.reshape(block_count, block_rows, width), table_of.reshape(block_count, block_rows)))
    attended = low(low_back(attended.reshape(group_rows, width)))
    branch = low_back(jnp.dot(attended, w_out, precision=HIGH) + b_out)
    out_one = layer_norm(encoded + branch, gain_one, shift_one)
    pre_act = low_back(jnp.dot(low(out_one), w_up, precision=HIGH) + b_up)
    activ = low(jax.nn.gelu(pre_act, approximate=False))
    ffn = low_back(jnp.dot(activ, w_down, precision=HIGH) + b_down)
    return layer_norm(out_one + ffn, gain_two, shift_two)

def reference(features, lengths, train_counts, used_features, w_enc, b_enc, w_qkv, b_query, b_value, w_out, b_out, gain_one, shift_one, w_up, b_up, w_down, b_down, gain_two, shift_two, cotangent):
    params = (w_enc.astype(jnp.float32), b_enc.astype(jnp.float32), w_qkv.astype(jnp.float32), b_query.astype(jnp.float32), b_value.astype(jnp.float32), w_out.astype(jnp.float32), b_out.astype(jnp.float32), gain_one.astype(jnp.float32), shift_one.astype(jnp.float32), w_up.astype(jnp.float32), b_up.astype(jnp.float32), w_down.astype(jnp.float32), b_down.astype(jnp.float32), gain_two.astype(jnp.float32), shift_two.astype(jnp.float32))
    feat_groups = features.astype(jnp.float32).reshape(GROUPS, TOK_GRP, F)
    cot_groups = cotangent.astype(jnp.float32).reshape(GROUPS, TOK_GRP, E)

    def one_group(totals, item):
        values, table_len, train_count, used_count, grad_out = item
        member, is_train, table_of = layout(table_len, train_count, TOK_GRP)

        def run(inputs, weights):
            return forward(inputs, weights, member, is_train, table_of, train_count, used_count)
        result, pull = jax.vjp(run, values, params)
        grad_values, grad_params = pull(grad_out)
        totals = jax.tree.map(lambda a, b: a + b, totals, grad_params)
        return (totals, (result.astype(jnp.bfloat16), grad_values))
    zeros = jax.tree.map(jnp.zeros_like, params)
    totals, (outputs, grads) = lax.scan(one_group, zeros, (feat_groups, lengths, train_counts, used_features, cot_groups))
    return (outputs.reshape(TOKENS, E), grads.reshape(TOKENS, F), totals[0], totals[1], totals[2], totals[3], totals[4], totals[5], totals[6], totals[7], totals[8], totals[9], totals[10], totals[11], totals[12], totals[13], totals[14])
```

```python
import functools
import math

import jax
import jax.numpy as jnp
from jax import lax
from jax.experimental import pallas as pl
from jax.experimental.pallas import tpu as pltpu
from jax.sharding import PartitionSpec as P

HEADS = 4
HD = 128
FEATS = 100
EPS = 1e-5
LOG2E = 1.4426950408889634
BIG = 1e30
SLOTS = 8
VMEM_BYTES = 58 * 1024 * 1024

BF = jnp.bfloat16
F32 = jnp.float32
MESH = pl.DeviceIdType.MESH


def dot(a, b):
    return lax.dot_general(a, b, (((1,), (0,)), ((), ())), preferred_element_type=F32)


def dot_nt(a, b):
    return lax.dot_general(a, b, (((1,), (1,)), ((), ())), preferred_element_type=F32)


def dot_tn(a, b):
    return lax.dot_general(a, b, (((0,), (0,)), ((), ())), preferred_element_type=F32)


def split3(v):
    high = v.astype(BF)
    rest = v - high.astype(F32)
    mid = rest.astype(BF)
    return high, mid, (rest - mid.astype(F32)).astype(BF)


def dot_split(v, b):
    high, mid, small = split3(v)
    return dot(high, b) + dot(mid, b) + dot(small, b)


def aug_lanes(base, value):
    high, mid, small = (part.astype(F32) for part in split3(value))
    lane = lax.broadcasted_iota(jnp.int32, base.shape, 1)
    out = jnp.where(lane == SLOTS, high, base.astype(F32))
    out = jnp.where(lane == SLOTS + 1, mid, out)
    return jnp.where(lane == SLOTS + 2, small, out).astype(BF)

def bits_below(count):
    return [1 << i for i in range(count.bit_length() - 1)]


def bit_of(index, bit):
    return lax.rem(index // bit, 2)


def flip(index, bit):
    return index + bit * (1 - 2 * bit_of(index, bit))


def greet(peers):
    barrier = pltpu.get_barrier_semaphore()
    for peer in peers:
        pl.semaphore_signal(barrier, inc=1, device_id=peer, device_id_type=MESH)
    pl.semaphore_wait(barrier, len(peers))


def send(src, dst, sems, slot, peer):
    return pltpu.make_async_remote_copy(
        src_ref=src, dst_ref=dst, send_sem=sems[0].at[slot], recv_sem=sems[1].at[slot],
        device_id=peer, device_id_type=MESH,
    )


def gather_feat(mine, full, sems, first, feat_count):
    me = lax.axis_index("feat")
    block = mine.shape[0]

    def at(index):
        return full.at[pl.ds(pl.multiple_of(index * block, block), block)]

    order = bits_below(feat_count)[::-1]
    steps = []
    held = [()]
    for bit in order:
        for path in held:
            steps.append((path, bit))
        held = held + [path + (bit,) for path in held]

    def make(number):
        path, bit = steps[number]
        index = me
        for done in path:
            index = flip(index, done)
        src = mine if not path else at(index)
        return send(src, at(index), sems, first + number, {"feat": flip(me, bit)})

    own = [n for n, (path, _) in enumerate(steps) if not path]
    for number in own:
        make(number).start()

    def finish():
        full[pl.ds(pl.multiple_of(me * block, block), block), :] = mine[...]
        for number, (path, _) in enumerate(steps):
            if path:
                make(number).start()
            make(number).wait_recv()
        for number in range(len(steps)):
            make(number).wait_send()

    return finish, len(steps)


def chunked(items, size):
    return [items[i : i + size] for i in range(0, len(items), size)]


class AllReduce:
    def __init__(self, x, out, work, first_in, later_in, sems, places, parts, group):
        self.x, self.out, self.work = x, out, work
        self.first_in, self.later_in, self.sems = first_in, later_in, sems
        self.place = {axis: lax.axis_index(axis) for axis in places}
        self.core = bit_of(self.place["feat"], 1)
        groups = chunked(reduce_bits(places), group)
        self.depth = len(groups)
        self.parts = []
        self.count = 2
        start = 0
        for number, size in enumerate(parts):
            turn = number * len(groups) // len(parts)
            at, landing, levels = start, start, []
            length = size
            for bits in groups[turn:] + groups[:turn]:
                length = length // 2 ** len(bits)
                member = sum(self.bit(b) << i for i, b in enumerate(bits))
                peers = []
                for subset in range(1, 2 ** len(bits)):
                    theirs = member
                    where = dict(self.place)
                    for i, (axis, bit) in enumerate(bits):
                        if subset >> i & 1:
                            theirs = theirs + (1 - 2 * self.bit((axis, bit))) * 2**i
                            where[axis] = flip(where[axis], bit)
                    peers.append((where, at + theirs * length, landing, self.count))
                    landing += length
                    self.count += 2
                at = at + member * length
                levels.append((peers, at, length))
            self.parts.append(levels)
            start += size

    def bit(self, which):
        return bit_of(self.place[which[0]], which[1])

    def rows(self, at, size):
        return pl.ds(pl.multiple_of(at, 16), size)

    def core_in(self):
        return send(self.x.at[1 - self.core], self.first_in, self.sems, 0, self.peers()[0])

    def core_out(self):
        half = self.out.at[self.core]
        return send(half, half, self.sems, 1, self.peers()[0])

    def down(self, part, level):
        peers, _, size = self.parts[part][level]
        return [
            send(
                self.work.at[self.rows(at, size)], self.later_in.at[pl.ds(landing, size)],
                self.sems, slot, where,
            )
            for where, at, landing, slot in peers
        ]

    def up(self, part, level):
        peers, at, size = self.parts[part][level]
        seg = self.out.at[self.core, self.rows(at, size)]
        return [send(seg, seg, self.sems, slot + 1, where) for where, _, _, slot in peers]

    def stage(self, number):
        depth = self.depth
        everyone = range(len(self.parts))
        if number == 0:
            self.core_in().start()
        elif number == 1:
            self.core_in().wait()
            total = self.x[self.core].astype(F32) + self.first_in[...].astype(F32)
            self.work[...] = total.astype(BF)
            for part in everyone:
                start_all(self.down(part, 0))
        elif number <= depth + 1:
            level = number - 2
            for part in everyone:
                wait_all(self.down(part, level))
                peers, at, size = self.parts[part][level]
                total = self.work[self.rows(at, size), :].astype(F32)
                for _, _, landing, _ in peers:
                    total = total + self.later_in[landing : landing + size, :].astype(F32)
                if level + 1 < depth:
                    self.work[self.rows(at, size), :] = total.astype(BF)
                    start_all(self.down(part, level + 1))
                else:
                    self.out[self.core, self.rows(at, size), :] = total.astype(BF)
                    start_all(self.up(part, level))
        elif number <= 2 * depth + 1:
            level = depth - 1 - (number - depth - 2)
            for part in everyone:
                wait_all(self.up(part, level))
                if level > 0:
                    start_all(self.up(part, level - 1))
            if level == 0:
                self.core_out().start()
        else:
            self.core_out().wait()

    @property
    def stages(self):
        return 2 * self.depth + 3

    def peers(self):
        first = dict(self.place)
        first["feat"] = flip(first["feat"], 1)
        return [first] + [where for peers, _, _ in self.parts[0] for where, _, _, _ in peers]


def start_all(copies):
    for copy in copies:
        copy.start()


def wait_all(copies):
    for copy in copies:
        copy.wait()


def reduce_bits(places):
    return [("feat", b) for b in bits_below(places["feat"])[1:]] + [
        ("rows", b) for b in bits_below(places["rows"])
    ]


def reduce_plan(rows_needed, places, group):
    bits = reduce_bits(places)
    groups = chunked(bits, group)
    granule = 16 * 2 ** len(bits)
    units = -(-rows_needed // granule)
    first = -(-units * 2 // 3)
    parts = [first, units - first] if len(groups) > 1 and units > 1 else [units]
    parts = [size * granule for size in parts]
    sems = 2 + 2 * len(parts) * sum(2 ** len(g) - 1 for g in groups)
    landing = sum(parts)
    return sum(parts), parts, sems, landing


def tail_kernel(
    x, grad, features_t, memt, trt, tab, stats,
    out, grad_x,
    mine, held, grad_in, work, first_in, later_in, send_s, recv_s, gsend_s, grecv_s,
    *, places, parts, group,
):
    me = lax.axis_index("feat")
    feat_count = places["feat"]
    reduce = AllReduce(
        x, out, work, first_in, later_in, (send_s, recv_s), places, parts, group
    )
    greet(reduce.peers())
    order = bits_below(feat_count)
    slots, number = {}, 0
    for bit in order:
        for i in range(feat_count // (2 * bit)):
            slots[bit, i] = number
            number += 1

    def copy(bit, i):
        j = 1 - bit_of(me, bit) + 2 * i
        src = grad.at[j] if bit == 1 else held.at[slots[bit // 2, 0] + j]
        return send(
            src, grad_in.at[slots[bit, i]], (gsend_s, grecv_s), slots[bit, i],
            {"feat": flip(me, bit)},
        )

    for i in range(feat_count // 2):
        copy(1, i).start()
    reduce.stage(0)
    for level, bit in enumerate(order):
        for i in range(feat_count // (2 * bit)):
            copy(bit, i).wait()
            j = bit_of(me, bit) + 2 * i
            here = grad[j] if bit == 1 else held[slots[bit // 2, 0] + j]
            total = here.astype(F32) + grad_in[slots[bit, i]].astype(F32)
            if level + 1 < len(order):
                held[slots[bit, i]] = total.astype(BF)
            else:
                mine[...] = total
        if level + 1 < len(order):
            for i in range(feat_count // (4 * bit)):
                copy(2 * bit, i).start()
        if level == 0:
            reduce.stage(1)

    cols_mine, rows = features_t.shape
    mean, var, factor = (stats[i, pl.ds(pl.multiple_of(me * cols_mine, 8), cols_mine), :] for i in range(3))
    count = tab[0:1, :]
    step = 512
    pieces = [slice(at, at + step) for at in range(0, rows, step)]

    def gather(v, member):
        high, mid, small = split3(v)
        return dot_nt(high, member) + dot_nt(mid, member) + dot_nt(small, member)

    d_factor = jnp.zeros((cols_mine, SLOTS), F32)
    for cut in pieces:
        c = features_t[:, cut].astype(F32) - dot_split(mean, memt[:, cut])
        grad_x[:, cut] = c
        d_factor = d_factor + gather(mine[:, cut] * c, memt[:, cut])
    reduce.stage(2)
    side = jnp.where(var > 0.25, 1.0, jnp.where(var == 0.25, 0.5, 0.0))
    d_var = d_factor * (-0.5) * factor / jnp.maximum(var, 0.25) * side
    pull = 2.0 * d_var / count
    d_mean = jnp.zeros((cols_mine, SLOTS), F32)
    for cut in pieces:
        dc = mine[:, cut] * dot_split(factor, memt[:, cut]) + grad_x[:, cut] * dot_split(
            pull, trt[:, cut]
        )
        grad_x[:, cut] = dc
        d_mean = d_mean - gather(dc, memt[:, cut])
    reduce.stage(3)
    d_mean = d_mean / count
    for cut in pieces:
        grad_x[:, cut] = grad_x[:, cut] + dot_split(d_mean, trt[:, cut])
    for number in range(4, reduce.stages):
        reduce.stage(number)


def prep_kernel(
    x_mine, w_mine, memt, trt, tab, b_enc, w_qkv, b_query, b_value,
    w_enc, stats, normed, normed_t, w_low, keys, vals, query, enc,
    xt, w_pair, cent, send_s, recv_s, *, rows_mine, feat_count,
):
    me = lax.axis_index("feat")
    greet([{"feat": flip(me, bit)} for bit in bits_below(feat_count)])
    end_x, used = gather_feat(x_mine, xt, (send_s, recv_s), 0, feat_count)
    end_w, _ = gather_feat(w_mine, w_enc, (send_s, recv_s), used, feat_count)
    columns, rows = xt.shape
    width = w_enc.shape[1]
    end_w()
    w_prod = dot(w_enc[...], w_qkv[...])
    high, mid, _ = split3(w_prod)
    w_pair[0:columns, :] = high
    w_pair[columns:, :] = mid
    w_low[...] = high
    bias = dot_split(jnp.broadcast_to(b_enc[...], (8, width)), w_qkv[...])[0:1, :]
    end_x()
    step = 512
    row_lo = pl.multiple_of(lax.axis_index("feat") * rows_mine, rows_mine)
    count = tab[0:1, :]
    sums = jnp.zeros((columns, SLOTS), F32)
    for at in range(0, rows, step):
        sums = sums + dot_nt(xt[:, at : at + step], trt[:, at : at + step])
    mean = sums / count
    var = jnp.zeros((columns, SLOTS), F32)
    for at in range(0, rows, step):
        member = memt[:, at : at + step]
        train = trt[:, at : at + step]
        c = xt[:, at : at + step].astype(F32) - dot_split(mean, member)
        cent[:, at : at + step] = c
        sq = c * c
        high, mid, _ = split3(sq)
        var = var + (dot_nt(high, train) + dot_nt(mid, train))
    var = var / count
    column = lax.broadcasted_iota(jnp.int32, (columns, SLOTS), 0).astype(F32)
    keep = column < tab[2:3, :]
    factor = jnp.where(keep, lax.rsqrt(jnp.maximum(var, 0.25)) * tab[1:2, :], 0.0)
    stats[0] = mean
    stats[1] = var
    stats[2] = factor

    for at in range(0, rows, step):
        member = memt[:, at : at + step]
        nt = cent[:, at : at + step] * dot_split(factor, member)
        normed_t[:, at : at + step] = nt.astype(BF)
        n = nt.T.astype(BF)
        normed[at : at + step, :] = n
        both = jnp.concatenate([n, n], axis=1)
        keys[at : at + step, :] = (
            dot(both, w_pair[:, width : 2 * width]) + bias[:, width : 2 * width]
        ).astype(BF)
        vals[at : at + step, :] = (
            dot(both, w_pair[:, 2 * width :]) + (bias[:, 2 * width :] + b_value[...])
        ).astype(BF)
    scale = LOG2E / math.sqrt(HD)
    step = min(256, rows_mine)
    for at in range(0, rows_mine, step):
        n = normed[pl.ds(row_lo + at, step), :]
        both = jnp.concatenate([n, n], axis=1)
        query[at : at + step, :] = (
            (dot(both, w_pair[:, 0:width]) + (bias[:, 0:width] + b_query[...])) * scale
        ).astype(BF)
        enc[at : at + step, :] = dot(n, w_enc[...]) + b_enc[...]


def tile_lanes(v, wide):
    return jnp.concatenate([v] * (wide // v.shape[1]), axis=1)


def forward_kernel(query, keys, vals, key_aug, query_tab, att, query_aug, acc, peak):
    rows_mine = query.shape[0]
    rows = keys.shape[0]
    q_step = min(256, rows_mine)
    k_step = 512
    ones = jnp.ones((k_step, HD), BF)

    @pl.loop(0, rows_mine // q_step)
    def _(block):
        q_rows = pl.ds(pl.multiple_of(block * q_step, q_step), q_step)
        table = query_tab[q_rows, :]
        for head in range(HEADS):
            acc[head] = jnp.zeros((q_step, 2 * HD), F32)
            peak[head] = jnp.full((q_step, HD), -3e38, F32)

        @pl.loop(0, rows // k_step)
        def _(chunk):
            k_rows = pl.ds(pl.multiple_of(chunk * k_step, k_step), k_step)
            aug = key_aug[k_rows, :]
            for head in range(HEADS):
                lanes = slice(head * HD, (head + 1) * HD)
                q = jnp.concatenate([query[q_rows, lanes], table], axis=1)
                k = jnp.concatenate([keys[k_rows, lanes], aug], axis=1)
                s = dot_nt(q, k)
                old = peak[head]
                new = jnp.maximum(old, jnp.max(s, axis=1, keepdims=True))
                peak[head] = new
                p = jnp.exp2(s - tile_lanes(new, k_step)).astype(BF)
                v = jnp.concatenate([vals[k_rows, lanes], ones], axis=1)
                alpha = tile_lanes(jnp.exp2(old - new), 2 * HD)
                acc[head] = acc[head] * alpha + dot(p, v)

        for head in range(HEADS):
            lanes = slice(head * HD, (head + 1) * HD)
            total = acc[head]
            norm = total[:, HD:]
            att[q_rows, lanes] = total[:, :HD] / norm
            query_aug[head, q_rows, :] = aug_lanes(table, -(peak[head] + jnp.log2(norm)))


def ffn_kernel(
    enc, att, normed, cot, w_out, b_out, gain_one, shift_one, w_up, b_up, w_down, b_down,
    gain_two, shift_two,
    out, grad_res, grad_att, att_aug, packed,
    small, attl_s, gbl_s, o1_s, gpre_s, act_s, gffn_s, nm_s, *, rows_mine,
):
    width = enc.shape[1]
    hidden = w_up.shape[1]
    step = min(256, rows_mine)
    row_lo = pl.multiple_of(lax.axis_index("feat") * rows_mine, rows_mine)
    small[...] = jnp.zeros(small.shape, F32)

    def add_small(slot, value, wide):
        small[slot : slot + 1, 0:wide] += jnp.sum(value, axis=0, keepdims=True)

    @pl.loop(0, rows_mine // step)
    def _(block):
        rows = pl.ds(pl.multiple_of(block * step, step), step)
        attended = att[rows, :]
        attl = attended.astype(BF)
        attl_s[rows, :] = attl
        resid = enc[rows, :] + dot(attl, w_out[...]) + b_out[...]
        ctr = resid - jnp.mean(resid, axis=1, keepdims=True)
        rstd1 = lax.rsqrt(jnp.mean(ctr * ctr, axis=1, keepdims=True) + EPS)
        n1 = ctr * rstd1
        o1 = n1 * gain_one[...] + shift_one[...]
        o1l = o1.astype(BF)
        o1_s[rows, :] = o1l
        pre = dot(o1l, w_up[...]) + b_up[...]
        cdf = 0.5 + 0.5 * lax.erf(pre * (1.0 / math.sqrt(2.0)))
        slope = cdf + pre * (jnp.exp(-0.5 * pre * pre) * (1.0 / math.sqrt(2.0 * math.pi)))
        actl = (pre * cdf).astype(BF)
        act_s[rows, :] = actl
        r2 = o1 + dot(actl, w_down[...]) + b_down[...]
        ctr2 = r2 - jnp.mean(r2, axis=1, keepdims=True)
        rstd2 = lax.rsqrt(jnp.mean(ctr2 * ctr2, axis=1, keepdims=True) + EPS)
        n2 = ctr2 * rstd2
        out[rows, :] = (n2 * gain_two[...] + shift_two[...]).astype(BF)
        go = cot[rows, :].astype(F32)
        add_small(0, go * n2, width)
        add_small(1, go, width)
        dn = go * gain_two[...]
        g2 = rstd2 * (
            dn - jnp.mean(dn, axis=1, keepdims=True) - n2 * jnp.mean(dn * n2, axis=1, keepdims=True)
        )
        gfl = g2.astype(BF)
        gffn_s[rows, :] = gfl
        add_small(2, g2, width)
        gpl = (dot_nt(gfl, w_down[...]) * slope).astype(BF)
        gpre_s[rows, :] = gpl
        add_small(3, gpl.astype(F32), hidden)
        g1 = dot_nt(gpl, w_up[...]) + g2
        add_small(4, g1 * n1, width)
        add_small(5, g1, width)
        dn1 = g1 * gain_one[...]
        gr = rstd1 * (
            dn1 - jnp.mean(dn1, axis=1, keepdims=True)
            - n1 * jnp.mean(dn1 * n1, axis=1, keepdims=True)
        )
        add_small(6, gr, width)
        gbl = gr.astype(BF)
        gbl_s[rows, :] = gbl
        grad_res[rows, :] = gbl
        ga = dot_nt(gbl, w_out[...]).astype(BF)
        grad_att[rows, :] = ga
        prod = ga.astype(F32) * attended
        zero = jnp.zeros((step, HD), BF)
        for head in range(HEADS):
            lanes = slice(head * HD, (head + 1) * HD)
            row_sum = jnp.sum(prod[:, lanes], axis=1, keepdims=True)
            att_aug[head, rows, :] = aug_lanes(zero, jnp.broadcast_to(-row_sum, (step, HD)))

    nm_s[...] = normed[pl.ds(row_lo, rows_mine), :]
    tile = 256
    half = width // 2

    def pack(at, value):
        rows = slice(at, at + value.shape[0])
        packed[0, rows, :] = value[:, :half].astype(BF)
        packed[1, rows, :] = value[:, half:].astype(BF)

    for at in range(0, width, tile):
        cut = slice(at, at + tile)
        pack(at, dot_tn(attl_s[:, cut], gbl_s[...]))
    base = width
    for at in range(0, width, tile):
        cut = slice(at, at + tile)
        up = dot_tn(o1_s[:, cut], gpre_s[...])
        for part in range(hidden // width):
            pack(base + part * width + at, up[:, part * width : (part + 1) * width])
    base = base + hidden
    for at in range(0, hidden, tile):
        cut = slice(at, at + tile)
        pack(base + at, dot_tn(act_s[:, cut], gffn_s[...]))
    base = base + hidden
    pack(base, dot_tn(nm_s[...], gbl_s[...]))
    base = base + normed.shape[1]
    pack(base, jnp.concatenate([small[:, :width], small[:, width:]], axis=0))
    base = base + 16
    if base < packed.shape[1]:
        packed[:, base:, :] = jnp.zeros((2, packed.shape[1] - base, half), BF)


def backward_kernel(
    query, query_aug, grad_att, att_aug, keys, vals, key_aug, normed_t, w_low, w_enc, grad_res,
    early, grad_low, late, early_out,
    grad_normed, moment, colsum, dq, dkv, work, first_in, later_in, send_s, recv_s,
    *, rows_mine, places, parts, group,
):
    reduce = AllReduce(
        early, early_out, work, first_in, later_in, (send_s, recv_s), places, parts, group
    )
    greet(reduce.peers())
    rows, width = keys.shape
    columns = normed_t.shape[0]
    k_step = 512
    slots = (0, 1, 5, 8, 11, 15)
    slots = slots[: min(len(slots), reduce.stages)]
    row_lo = pl.multiple_of(lax.axis_index("feat") * rows_mine, rows_mine)
    dq[...] = jnp.zeros(dq.shape, F32)
    moment[...] = jnp.zeros(moment.shape, F32)
    colsum[...] = jnp.zeros(colsum.shape, F32)

    @pl.loop(0, rows // k_step)
    def _(chunk):
        k_rows = pl.ds(pl.multiple_of(chunk * k_step, k_step), k_step)
        aug = key_aug[k_rows, :]
        for head in range(HEADS):
            lanes = slice(head * HD, (head + 1) * HD)
            q = query[:, lanes]
            k = keys[k_rows, lanes]
            do = grad_att[:, lanes]
            s = dot_nt(
                jnp.concatenate([k, aug], axis=1),
                jnp.concatenate([q, query_aug[head]], axis=1),
            )
            p = jnp.exp2(s)
            dp = dot_nt(
                jnp.concatenate([vals[k_rows, lanes], aug], axis=1),
                jnp.concatenate([do, att_aug[head]], axis=1),
            )
            ds = (p * dp).astype(BF)
            dv = dot(p.astype(BF), do)
            dk = dot(ds, q) * (1.0 / LOG2E)
            dkv[:, lanes] = dk.astype(BF)
            dkv[:, width + head * HD : width + (head + 1) * HD] = dv.astype(BF)
            colsum[0:1, width + head * HD : width + (head + 1) * HD] += jnp.sum(
                dk, axis=0, keepdims=True
            )
            colsum[0:1, 2 * width + head * HD : 2 * width + (head + 1) * HD] += jnp.sum(
                dv, axis=0, keepdims=True
            )
            dq[:, lanes] += dot_tn(ds, k)
            if head % 2 == 1:
                for number, when in enumerate(slots):

                    @pl.when(2 * chunk + head // 2 == when)
                    def _(number=number):
                        reduce.stage(number)

        grads = dkv[...]
        moment[:, width:] += dot(normed_t[:, k_rows], grads)
        grad_normed[:, k_rows] = dot_nt(w_low[:, width:], grads)

    dql = (dq[...] * (1.0 / math.sqrt(HD))).astype(BF)
    mine = pl.ds(row_lo, rows_mine)
    colsum[0:1, 0:width] = jnp.sum(dql.astype(F32), axis=0, keepdims=True)
    moment[:, 0:width] = dot(normed_t[:, mine], dql)
    grad_normed[:, mine] += dot_nt(w_low[:, 0:width], dql) + dot_nt(w_enc[...], grad_res[...])
    grad_low[...] = grad_normed[...].astype(BF)
    half = width // 2
    late[...] = jnp.zeros(late.shape, BF)
    for part in range(3):
        for side in range(2):
            lanes = slice(part * width + side * half, part * width + (side + 1) * half)
            late[side, part * columns : (part + 1) * columns, :] = moment[:, lanes].astype(BF)
            at = 3 * columns + 16 * part
            late[side, at : at + 16, :] = jnp.concatenate(
                [colsum[:, lanes], jnp.zeros((8, half), F32)], axis=0
            ).astype(BF)
    for number in range(len(slots), reduce.stages):
        reduce.stage(number)


def vmem(count):
    return [pl.BlockSpec(memory_space=pltpu.VMEM)] * count


def call(kernel, outs, scratch, args, **params):
    return pl.pallas_call(
        kernel,
        out_shape=tuple(jax.ShapeDtypeStruct(shape, kind) for shape, kind in outs),
        in_specs=vmem(len(args)),
        out_specs=tuple(vmem(len(outs))),
        scratch_shapes=[
            pltpu.SemaphoreType.DMA((entry,)) if isinstance(entry, int) else pltpu.VMEM(*entry)
            for entry in scratch
        ],
        compiler_params=pltpu.CompilerParams(vmem_limit_bytes=VMEM_BYTES, **params),
    )(*args)


def per_device(
    features, lengths, train_counts, used_features, w_enc, b_enc, w_qkv, b_query, b_value,
    w_out, b_out, gain_one, shift_one, w_up, b_up, w_down, b_down, gain_two, shift_two, cotangent,
):
    feat_count = lax.axis_size("feat")
    feat_index = lax.axis_index("feat")
    rows, cols_mine = features.shape
    columns = cols_mine * feat_count
    width = w_qkv.shape[0]
    hidden = w_up.shape[1]
    rows_mine = rows // feat_count
    tables = lengths.shape[1]

    def pad(v, fill):
        return jnp.pad(v, ((0, SLOTS - tables),), constant_values=fill)

    table_len, train_count, used = lengths[0], train_counts[0], used_features[0]
    ends = jnp.cumsum(table_len)
    starts = pad(ends - table_len, rows)
    stops = pad(ends, rows)
    learned = pad(ends - table_len + train_count, rows)
    at = jnp.arange(rows, dtype=jnp.int32)[None, :]
    member = (at >= starts[:, None]) & (at < stops[:, None])
    train = member & (at < learned[:, None])
    mem_t = member.astype(BF)
    tr_t = train.astype(BF)
    used_f = pad(used, 1).astype(F32)
    tab = jnp.stack(
        [pad(train_count, 1).astype(F32), jnp.sqrt(FEATS / used_f), pad(used, 0).astype(F32)]
        + [jnp.zeros((SLOTS,), F32)] * 5
    )
    key_aug = jnp.concatenate(
        [
            jnp.where(train.T, 0.0, -BIG).astype(BF),
            jnp.ones((rows, 3), BF),
            jnp.zeros((rows, HD - SLOTS - 3), BF),
        ],
        axis=1,
    )
    query_tab = jnp.pad(
        lax.dynamic_slice_in_dim(mem_t, feat_index * rows_mine, rows_mine, axis=1).T,
        ((0, 0), (0, HD - SLOTS)),
    )

    features_t = features.T
    places = {"feat": feat_count, "rows": lax.axis_size("rows")}
    half = width // 2

    row = lambda v: v.reshape(1, -1)
    gather_sems = 2 * (feat_count - 1)
    w_enc_all, stats, normed, normed_t, w_low, keys, vals, query, enc = call(
        functools.partial(prep_kernel, rows_mine=rows_mine, feat_count=feat_count),
        [
            ((columns, width), BF), ((3, columns, SLOTS), F32), ((rows, columns), BF),
            ((columns, rows), BF), ((columns, 3 * width), BF), ((rows, width), BF),
            ((rows, width), BF), ((rows_mine, width), BF), ((rows_mine, width), F32),
        ],
        [
            ((columns, rows), BF), ((2 * columns, 3 * width), BF), ((columns, rows), F32),
            gather_sems, gather_sems,
        ],
        (features_t, w_enc, mem_t, tr_t, tab, row(b_enc), w_qkv, row(b_query), row(b_value)),
        collective_id=0, has_side_effects=True,
    )
    q_step = min(256, rows_mine)
    att, query_aug = call(
        forward_kernel,
        [((rows_mine, width), F32), ((HEADS, rows_mine, HD), BF)],
        [((HEADS, q_step, 2 * HD), F32), ((HEADS, q_step, HD), F32)],
        (query, keys, vals, key_aug, query_tab),
    )
    early_rows, early_parts, early_sems, early_land = reduce_plan(
        width + 2 * hidden + columns + 16, places, 2
    )
    out, grad_res, grad_att, att_aug, early = call(
        functools.partial(ffn_kernel, rows_mine=rows_mine),
        [
            ((rows_mine, width), BF), ((rows_mine, width), BF), ((rows_mine, width), BF),
            ((HEADS, rows_mine, HD), BF), ((2, early_rows, half), BF),
        ],
        [
            ((8, hidden), F32),
            ((rows_mine, width), BF), ((rows_mine, width), BF), ((rows_mine, width), BF),
            ((rows_mine, hidden), BF), ((rows_mine, hidden), BF), ((rows_mine, width), BF),
            ((rows_mine, columns), BF),
        ],
        (
            enc, att, normed, cotangent, w_out, row(b_out), row(gain_one), row(shift_one), w_up,
            row(b_up), w_down, row(b_down), row(gain_two), row(shift_two),
        ),
    )
    late_rows, late_parts, late_sems, late_land = reduce_plan(3 * columns + 48, places, 4)
    grad_low, late, early = call(
        functools.partial(
            backward_kernel, rows_mine=rows_mine, places=places, parts=early_parts, group=2
        ),
        [((columns, rows), BF), ((2, late_rows, half), BF), ((2, early_rows, half), BF)],
        [
            ((columns, rows), F32), ((columns, 3 * width), F32), ((8, 3 * width), F32),
            ((rows_mine, width), F32), ((512, 2 * width), BF), ((early_rows, half), BF),
            ((early_rows, half), BF), ((early_land, half), BF), early_sems, early_sems,
        ],
        (
            query, query_aug, grad_att, att_aug, keys, vals, key_aug, normed_t, w_low, w_enc_all,
            grad_res, early,
        ),
        collective_id=1, has_side_effects=True,
    )
    late, grad_x = call(
        functools.partial(
            tail_kernel, places=places, parts=late_parts, group=4
        ),
        [((2, late_rows, half), BF), ((cols_mine, rows), F32)],
        [
            ((cols_mine, rows), F32), ((feat_count - 1, cols_mine, rows), BF),
            ((feat_count - 1, cols_mine, rows), BF), ((late_rows, half), BF),
            ((late_rows, half), BF), ((late_land, half), BF), late_sems, late_sems, feat_count - 1,
            feat_count - 1,
        ],
        (
            late, grad_low.reshape(feat_count, cols_mine, rows), features_t, mem_t, tr_t, tab,
            stats,
        ),
        collective_id=2, has_side_effects=True,
    )
    grad_features = grad_x.T

    def take(v, lo, count):
        return jnp.concatenate([v[0, lo : lo + count], v[1, lo : lo + count]], axis=1)

    base = width
    grad_w_out = take(early, 0, width).astype(F32)
    grad_w_up = jnp.concatenate(
        [take(early, base + i * width, width) for i in range(hidden // width)], axis=1
    ).astype(F32)
    base = base + hidden
    grad_w_down = take(early, base, hidden).astype(F32)
    base = base + hidden
    local = take(early, base, columns).astype(F32)
    small = take(early, base + columns, 16).astype(F32)
    moment = jnp.concatenate([take(late, i * columns, columns) for i in range(3)], axis=1)
    sums = jnp.concatenate([take(late, 3 * columns + 16 * i, 1)[0] for i in range(3)]).astype(F32)
    grad_w_qkv = (
        jnp.einsum("fe,fo->eo", w_enc_all, moment, preferred_element_type=F32)
        + b_enc[:, None] * sums[None, :]
    )
    grad_w_enc = lax.dynamic_slice_in_dim(
        jnp.einsum("fo,eo->fe", moment, w_qkv, preferred_element_type=F32) + local,
        feat_index * cols_mine, cols_mine, axis=0,
    )
    grad_b_enc = (
        jnp.einsum("o,eo->e", sums, w_qkv.astype(F32), precision=lax.Precision.HIGHEST) + small[6]
    )
    return (
        out, grad_features, grad_w_enc, grad_b_enc, grad_w_qkv, sums[:width], sums[2 * width :],
        grad_w_out, small[6], small[4], small[5], grad_w_up,
        jnp.concatenate([small[3], small[11]]), grad_w_down, small[2], small[0], small[1],
    )


def solution(mesh):
    whole = P()
    in_specs = (
        (P("rows", "feat"),) + (P("rows", None),) * 3 + (P("feat", None),) + (whole,) * 14
        + (P(("rows", "feat"), None),)
    )
    out_specs = (
        (P(("rows", "feat"), None), P("rows", "feat"), P("feat", None)) + (whole,) * 14
    )
    return jax.shard_map(
        per_device, mesh=mesh, in_specs=in_specs, out_specs=out_specs, check_vma=False
    )
```

```python
import functools
import math

import jax
import jax.numpy as jnp
from jax import lax
from jax.experimental import pallas as pl
from jax.experimental.pallas import tpu as pltpu
from jax.sharding import PartitionSpec as P

HEADS = 4
HD = 128
FEATS = 100
EPS = 1e-5
LOG2E = 1.4426950408889634
BIG = 1e30
SLOTS = 8
SLOTS_AT = (0, 4, 7, 10, 14)
VMEM_BYTES = 63 * 1024 * 1024

BF = jnp.bfloat16
F32 = jnp.float32
MESH = pl.DeviceIdType.MESH


def dot(a, b):
    return lax.dot_general(a, b, (((1,), (0,)), ((), ())), preferred_element_type=F32)


def dot_nt(a, b):
    return lax.dot_general(a, b, (((1,), (1,)), ((), ())), preferred_element_type=F32)


def dot_tn(a, b):
    return lax.dot_general(a, b, (((0,), (0,)), ((), ())), preferred_element_type=F32)


def split3(v):
    high = v.astype(BF)
    rest = v - high.astype(F32)
    mid = rest.astype(BF)
    return high, mid, (rest - mid.astype(F32)).astype(BF)


def dot_split(v, b):
    high, mid, small = split3(v)
    return dot(high, b) + dot(mid, b) + dot(small, b)


def aug_lanes(base, value):
    high, mid, small = (part.astype(F32) for part in split3(value))
    lane = lax.broadcasted_iota(jnp.int32, base.shape, 1)
    out = jnp.where(lane == SLOTS, high, base.astype(F32))
    out = jnp.where(lane == SLOTS + 1, mid, out)
    return jnp.where(lane == SLOTS + 2, small, out).astype(BF)

def bits_below(count):
    return [1 << i for i in range(count.bit_length() - 1)]


def bit_of(index, bit):
    return lax.rem(index // bit, 2)


def flip(index, bit):
    return index + bit * (1 - 2 * bit_of(index, bit))


def greet(peers):
    barrier = pltpu.get_barrier_semaphore()
    for peer in peers:
        pl.semaphore_signal(barrier, inc=1, device_id=peer, device_id_type=MESH)
    pl.semaphore_wait(barrier, len(peers))


def send(src, dst, sems, slot, peer):
    return pltpu.make_async_remote_copy(
        src_ref=src, dst_ref=dst, send_sem=sems[0].at[slot], recv_sem=sems[1].at[slot],
        device_id=peer, device_id_type=MESH,
    )


def gather_steps(feat_count):
    steps, held = [], [()]
    for bit in bits_below(feat_count)[::-1]:
        steps += [(path, bit) for path in held]
        held = held + [path + (bit,) for path in held]
    return steps


class GatherFeat:
    def __init__(self, full, block, piece, sems, first, feat_count):
        self.full, self.block, self.piece = full, block, piece
        self.sems, self.first = sems, first
        self.steps = gather_steps(feat_count)
        self.me = lax.axis_index("feat")
        self.waited = set()

    def copy(self, number, at):
        path, bit = self.steps[number]
        index = self.me
        for done in path:
            index = flip(index, done)
        part = self.full.at[
            pl.ds(pl.multiple_of(index * self.block, self.block), self.block),
            pl.ds(at * self.piece, self.piece),
        ]
        slot = self.first + at * len(self.steps) + number
        return send(part, part, self.sems, slot, {"feat": flip(self.me, bit)})

    def arrived(self, number, at):
        if (number, at) not in self.waited:
            self.waited.add((number, at))
            self.copy(number, at).wait_recv()

    def start(self, at):
        for number, (path, _) in enumerate(self.steps):
            if not path:
                self.copy(number, at).start()

    def forward(self, at):
        for number, (path, _) in enumerate(self.steps):
            if path:
                self.arrived(self.steps.index((path[:-1], path[-1])), at)
                self.copy(number, at).start()

    def finish(self, at):
        for number in range(len(self.steps)):
            self.arrived(number, at)
        for number in range(len(self.steps)):
            self.copy(number, at).wait_send()


def chunked(items, size):
    return [items[i : i + size] for i in range(0, len(items), size)]


class AllReduce:
    def __init__(self, x, out, first_in, later_in, sems, places, parts, group):
        self.x, self.out = x, out
        self.first_in, self.later_in, self.sems = first_in, later_in, sems
        self.place = {axis: lax.axis_index(axis) for axis in places}
        self.core = bit_of(self.place["feat"], 1)
        groups = chunked(reduce_bits(places), group)
        self.depth = len(groups)
        self.parts = []
        self.count = 2
        start = 0
        for number, size in enumerate(parts):
            turn = number * len(groups) // len(parts)
            at, landing, levels = start, start, []
            length = size
            for bits in groups[turn:] + groups[:turn]:
                length = length // 2 ** len(bits)
                member = sum(self.bit(b) << i for i, b in enumerate(bits))
                peers = []
                for subset in range(1, 2 ** len(bits)):
                    theirs = member
                    where = dict(self.place)
                    for i, (axis, bit) in enumerate(bits):
                        if subset >> i & 1:
                            theirs = theirs + (1 - 2 * self.bit((axis, bit))) * 2**i
                            where[axis] = flip(where[axis], bit)
                    peers.append((where, at + theirs * length, landing, self.count))
                    landing += length
                    self.count += 2
                at = at + member * length
                levels.append((peers, at, length))
            self.parts.append(levels)
            start += size

    def bit(self, which):
        return bit_of(self.place[which[0]], which[1])

    def rows(self, at, size):
        return pl.ds(pl.multiple_of(at, 16), size)

    def core_in(self):
        return send(self.x.at[1 - self.core], self.first_in, self.sems, 0, self.peers()[0])

    def core_out(self):
        half = self.out.at[self.core]
        return send(half, half, self.sems, 1, self.peers()[0])

    def down(self, part, level):
        peers, _, size = self.parts[part][level]
        return [
            send(
                self.x.at[self.core, self.rows(at, size)], self.later_in.at[pl.ds(landing, size)],
                self.sems, slot, where,
            )
            for where, at, landing, slot in peers
        ]

    def up(self, part, level):
        peers, at, size = self.parts[part][level]
        seg = self.out.at[self.core, self.rows(at, size)]
        return [send(seg, seg, self.sems, slot + 1, where) for where, _, _, slot in peers]

    def stage(self, number):
        depth = self.depth
        everyone = range(len(self.parts))
        if number == 0:
            self.core_in().start()
        elif number == 1:
            self.core_in().wait()
            total = self.x[self.core].astype(F32) + self.first_in[...].astype(F32)
            self.x[self.core] = total.astype(BF)
            for part in everyone:
                start_all(self.down(part, 0))
        elif number <= depth + 1:
            level = number - 2
            for part in everyone:
                wait_all(self.down(part, level))
                peers, at, size = self.parts[part][level]
                total = self.x[self.core, self.rows(at, size), :].astype(F32)
                for _, _, landing, _ in peers:
                    total = total + self.later_in[landing : landing + size, :].astype(F32)
                if level + 1 < depth:
                    self.x[self.core, self.rows(at, size), :] = total.astype(BF)
                    start_all(self.down(part, level + 1))
                else:
                    self.out[self.core, self.rows(at, size), :] = total.astype(BF)
                    start_all(self.up(part, level))
        elif number <= 2 * depth + 1:
            level = depth - 1 - (number - depth - 2)
            for part in everyone:
                wait_all(self.up(part, level))
                if level > 0:
                    start_all(self.up(part, level - 1))
            if level == 0:
                self.core_out().start()
        else:
            self.core_out().wait()

    @property
    def stages(self):
        return 2 * self.depth + 3

    def peers(self):
        first = dict(self.place)
        first["feat"] = flip(first["feat"], 1)
        return [first] + [where for peers, _, _ in self.parts[0] for where, _, _, _ in peers]


def start_all(copies):
    for copy in copies:
        copy.start()


def wait_all(copies):
    for copy in copies:
        copy.wait()


def reduce_bits(places):
    return [("feat", b) for b in bits_below(places["feat"])[1:]] + [
        ("rows", b) for b in bits_below(places["rows"])
    ]


def reduce_plan(rows_needed, places, group):
    bits = reduce_bits(places)
    groups = chunked(bits, group)
    granule = 16 * 2 ** len(bits)
    units = -(-rows_needed // granule)
    first = -(-units * 2 // 3)
    parts = [first, units - first] if len(groups) > 1 and units > 1 else [units]
    parts = [size * granule for size in parts]
    sems = 2 + 2 * len(parts) * sum(2 ** len(g) - 1 for g in groups)
    landing = sum(parts)
    return sum(parts), parts, sems, landing


def tile_lanes(v, wide):
    return jnp.concatenate([v] * (wide // v.shape[1]), axis=1)


def table_masks(refs, mem_t, tr_t, key_aug, tab):
    lengths, trains, used = refs
    tables = lengths.shape[1]
    slots, rows = mem_t.shape
    row = lax.broadcasted_iota(jnp.int32, (slots, rows), 0)
    at = lax.broadcasted_iota(jnp.int32, (slots, rows), 1)
    lane = lax.broadcasted_iota(jnp.int32, (1, HD), 1)
    slot = lax.broadcasted_iota(jnp.int32, (8, slots), 1)
    line = lax.broadcasted_iota(jnp.int32, (8, slots), 0)
    member = jnp.zeros((slots, rows), jnp.bool_)
    train = jnp.zeros((slots, rows), jnp.bool_)
    low = jnp.full((1, HD), rows, jnp.int32)
    high = jnp.full((1, HD), 0, jnp.int32)
    counts = jnp.where(line < 2, 1, 0)
    start = jnp.int32(0)
    for j in range(tables):
        stop = start + lengths[0, j]
        learned = start + trains[0, j]
        here = (row == j) & (at >= start)
        member = member | (here & (at < stop))
        train = train | (here & (at < learned))
        low = jnp.where(lane == j, start, low)
        high = jnp.where(lane == j, learned, high)
        counts = jnp.where((slot == j) & (line == 0), trains[0, j], counts)
        counts = jnp.where((slot == j) & (line > 0), used[0, j], counts)
        start = stop
    mem_t[...] = jnp.where(member, 1.0, 0.0).astype(BF)
    tr_t[...] = jnp.where(train, 1.0, 0.0).astype(BF)
    counts = counts.astype(F32)
    tab[...] = jnp.where(line[...] == 1, jnp.sqrt(FEATS / jnp.maximum(counts, 1.0)), counts)
    step = 512

    @pl.loop(0, rows // step)
    def _(block):
        token = lax.broadcasted_iota(jnp.int32, (step, HD), 0) + block * step
        wide = lax.broadcasted_iota(jnp.int32, (step, HD), 1)
        open_to = (token >= low) & (token < high)
        mask = jnp.where(wide < SLOTS, jnp.where(open_to, 0.0, -BIG), 0.0)
        ones = (wide >= SLOTS) & (wide < SLOTS + 3)
        key_aug[pl.ds(pl.multiple_of(block * step, step), step), :] = jnp.where(
            ones, 1.0, mask
        ).astype(BF)

    return start


def layer_kernel(
    lengths, trains, used, features_t, w_mine, b_enc, b_query, b_value, b_out, gain_one, shift_one,
    b_up, b_down, gain_two, shift_two,
    w_qkv_h, w_out_h, w_up_h, w_down_h, cot_h,
    out_h, early_h, late_out, grad_x, w_enc,
    w_out, w_up, w_down, cot,
    mem_t, tr_t, tab, key_aug, cent, normed_t, w_pair, keys, vals, query, enc, att,
    query_aug, grad_att, att_aug, sbuf,
    small, attl_s, gbl_s, o1_s, gffn_s, gpre_s, act_s,
    early_x, early_o, first_e, later_e, grad_low,
    late_x, first_l, later_l, held, grad_in,
    local_sem, gsend, grecv, esend, erecv, lsend, lrecv, rsend, rrecv,
    *, places, early_parts, early_group, late_parts, late_group,
):
    feat_count = places["feat"]
    me = lax.axis_index("feat")
    cols_mine, rows = features_t.shape
    columns, width = w_enc.shape
    hidden = w_up.shape[1]
    rows_mine = query.shape[0]
    row_lo = pl.multiple_of(me * rows_mine, rows_mine)
    col_lo = pl.multiple_of(me * cols_mine, cols_mine)
    half = width // 2

    early = AllReduce(
        early_x, early_o, first_e, later_e, (esend, erecv), places, early_parts, early_group
    )
    late = AllReduce(
        late_x, late_out, first_l, later_l, (lsend, lrecv), places, late_parts, late_group
    )
    w_qkv = [ref.at[0:width, :] for ref in (gbl_s, o1_s, gffn_s)]
    loads = [
        pltpu.make_async_copy(src, dst, local_sem.at[i])
        for i, (src, dst) in enumerate(
            [
                (w_qkv_h.at[:, pl.ds(part * width, width)], w_part)
                for part, w_part in enumerate(w_qkv)
            ]
            + [(cot_h, cot), (w_out_h, w_out), (w_up_h, w_up), (w_down_h, w_down)]
        )
    ]
    start_all(loads)
    greet(late.peers())

    w_enc[pl.ds(col_lo, cols_mine), :] = w_mine[...]
    steps = len(gather_steps(feat_count))
    gather_w = GatherFeat(w_enc, cols_mine, width, (gsend, grecv), 0, feat_count)
    gather_w.start(0)

    table_masks((lengths, trains, used), mem_t, tr_t, key_aug, tab)
    step = 512
    pieces = [slice(at, at + step) for at in range(0, rows, step)]
    count = tab[0:1, :]
    mean = jnp.zeros((cols_mine, SLOTS), F32)
    for cut in pieces:
        mean = mean + dot_nt(features_t[:, cut], tr_t[:, cut])
    mean = mean / count
    var = jnp.zeros((cols_mine, SLOTS), F32)
    for cut in pieces:
        c = features_t[:, cut].astype(F32) - dot_split(mean, mem_t[:, cut])
        cent[:, cut] = c
        high, mid, _ = split3(c * c)
        var = var + (dot_nt(high, tr_t[:, cut]) + dot_nt(mid, tr_t[:, cut]))
    var = var / count
    column = (lax.broadcasted_iota(jnp.int32, (cols_mine, SLOTS), 0) + col_lo).astype(F32)
    factor = jnp.where(
        column < tab[2:3, :], lax.rsqrt(jnp.maximum(var, 0.25)) * tab[1:2, :], 0.0
    )
    for cut in pieces:
        normed_t[pl.ds(col_lo, cols_mine), cut] = (
            cent[:, cut] * dot_split(factor, mem_t[:, cut])
        ).astype(BF)
    splits = 4
    piece = rows // splits
    gather_x = GatherFeat(normed_t, cols_mine, piece, (gsend, grecv), steps, feat_count)
    for at in range(splits):
        gather_x.start(at)

    gather_w.forward(0)
    gather_w.finish(0)
    wait_all(loads[:3])
    bias = []
    for part, w_part in enumerate(w_qkv):
        lanes = slice(part * width, (part + 1) * width)
        high, mid, _ = split3(dot(w_enc[...], w_part[...]))
        w_pair[0:columns, lanes] = high
        w_pair[columns:, lanes] = mid
        bias.append(dot_split(jnp.broadcast_to(b_enc[...], (8, width)), w_part[...])[0:1, :])
    bias_q, bias_k, bias_v = bias[0] + b_query[...], bias[1], bias[2] + b_value[...]

    def project(at):
        for lo in range(at * piece, (at + 1) * piece, step):
            n = normed_t[:, lo : lo + step].astype(F32).T.astype(BF)
            both = jnp.concatenate([n, n], axis=1)
            keys[lo : lo + step, :] = (
                dot(both, w_pair[:, width : 2 * width]) + bias_k
            ).astype(BF)
            vals[lo : lo + step, :] = (
                dot(both, w_pair[:, 2 * width :]) + bias_v
            ).astype(BF)

    gather_x.forward(0)
    for at in range(splits):
        if at + 1 < splits:
            gather_x.forward(at + 1)
        gather_x.finish(at)
        project(at)
    block = min(256, rows_mine)
    scale = LOG2E / math.sqrt(HD)
    for lo in range(0, rows_mine, block):
        cols = pl.ds(pl.multiple_of(row_lo + lo, block), block)
        n = normed_t[:, cols].astype(F32).T.astype(BF)
        both = jnp.concatenate([n, n], axis=1)
        query[lo : lo + block, :] = (
            (dot(both, w_pair[:, 0:width]) + bias_q) * scale
        ).astype(BF)
        enc[lo : lo + block, :] = dot(n, w_enc[...]) + b_enc[...]

    q_step = min(256, rows_mine)
    k_step = 512
    ones = jnp.ones((k_step, HD), BF)

    @pl.loop(0, rows_mine // q_step)
    def _(number):
        lo = pl.multiple_of(number * q_step, q_step)
        q_rows = pl.ds(lo, q_step)
        cols = pl.ds(pl.multiple_of(row_lo + lo, q_step), q_step)
        table = jnp.concatenate(
            [mem_t[:, cols].astype(F32), jnp.zeros((HD - SLOTS, q_step), F32)], axis=0
        ).T.astype(BF)
        for head in range(HEADS):
            lanes = slice(head * HD, (head + 1) * HD)
            q = jnp.concatenate([query[q_rows, lanes], table], axis=1)
            peak = jnp.full((q_step, HD), -3e38, F32)
            for at in range(0, rows, k_step):
                k_rows = slice(at, at + k_step)
                k = jnp.concatenate([keys[k_rows, lanes], key_aug[k_rows, :]], axis=1)
                s = dot_nt(q, k)
                sbuf[head % 2, :, k_rows] = s
                for lo in range(0, k_step, HD):
                    peak = jnp.maximum(peak, s[:, lo : lo + HD])
            top = jnp.broadcast_to(jnp.max(peak, axis=1, keepdims=True), (q_step, HD))
            total = jnp.zeros((q_step, 2 * HD), F32)
            for at in range(0, rows, k_step):
                k_rows = slice(at, at + k_step)
                p = jnp.exp2(sbuf[head % 2, :, k_rows] - tile_lanes(top, k_step)).astype(BF)
                v = jnp.concatenate([vals[k_rows, lanes], ones], axis=1)
                total = total + dot(p, v)
            norm = total[:, HD:]
            att[q_rows, lanes] = total[:, :HD] / norm
            query_aug[head, q_rows, :] = aug_lanes(table, -(top + jnp.log2(norm)))

    wait_all(loads[3:])
    small[...] = jnp.zeros(small.shape, F32)

    def add_small(slot, value, wide):
        small[slot : slot + 1, 0:wide] += jnp.sum(value, axis=0, keepdims=True)

    def mean_of(v):
        return jnp.mean(v, axis=1, keepdims=True)

    @pl.loop(0, rows_mine // block)
    def _(number):
        at = pl.ds(pl.multiple_of(number * block, block), block)
        attended = att[at, :]
        attl = attended.astype(BF)
        attl_s[at, :] = attl
        resid = enc[at, :] + dot(attl, w_out[...]) + b_out[...]
        ctr = resid - mean_of(resid)
        rstd1 = lax.rsqrt(mean_of(ctr * ctr) + EPS)
        n1 = ctr * rstd1
        o1 = n1 * gain_one[...] + shift_one[...]
        o1l = o1.astype(BF)
        o1_s[at, :] = o1l
        pre = dot(o1l, w_up[...]) + b_up[...]
        cdf = 0.5 + 0.5 * lax.erf(pre * (1.0 / math.sqrt(2.0)))
        slope = cdf + pre * (jnp.exp(-0.5 * pre * pre) * (1.0 / math.sqrt(2.0 * math.pi)))
        actl = (pre * cdf).astype(BF)
        act_s[at, :] = actl
        r2 = o1 + dot(actl, w_down[...]) + b_down[...]
        ctr2 = r2 - mean_of(r2)
        rstd2 = lax.rsqrt(mean_of(ctr2 * ctr2) + EPS)
        n2 = ctr2 * rstd2
        go = cot[at, :].astype(F32)
        cot[at, :] = (n2 * gain_two[...] + shift_two[...]).astype(BF)
        add_small(0, go * n2, width)
        add_small(1, go, width)
        dn = go * gain_two[...]
        g2 = rstd2 * (dn - mean_of(dn) - n2 * mean_of(dn * n2))
        gfl = g2.astype(BF)
        gffn_s[at, :] = gfl
        add_small(2, g2, width)
        gpl = (dot_nt(gfl, w_down[...]) * slope).astype(BF)
        gpre_s[at, :] = gpl
        add_small(3, gpl.astype(F32), hidden)
        g1 = dot_nt(gpl, w_up[...]) + g2
        add_small(4, g1 * n1, width)
        add_small(5, g1, width)
        dn1 = g1 * gain_one[...]
        gr = rstd1 * (dn1 - mean_of(dn1) - n1 * mean_of(dn1 * n1))
        add_small(6, gr, width)
        gbl = gr.astype(BF)
        gbl_s[at, :] = gbl
        ga = dot_nt(gbl, w_out[...]).astype(BF)
        grad_att[at, :] = ga
        prod = ga.astype(F32) * attended
        zero = jnp.zeros((block, HD), BF)
        for head in range(HEADS):
            lanes = slice(head * HD, (head + 1) * HD)
            row_sum = jnp.sum(prod[:, lanes], axis=1, keepdims=True)
            att_aug[head, at, :] = aug_lanes(zero, jnp.broadcast_to(-row_sum, (block, HD)))

    store_out = pltpu.make_async_copy(cot, out_h, local_sem.at[7])
    store_out.start()

    def pack(at, value):
        into = slice(at, at + value.shape[0])
        early_x[0, into, :] = value[:, :half].astype(BF)
        early_x[1, into, :] = value[:, half:].astype(BF)

    own = pl.ds(row_lo, rows_mine)
    tile = 256
    for at in range(0, width, tile):
        pack(at, dot_tn(attl_s[:, at : at + tile], gbl_s[...]))
    base = width
    for at in range(0, width, tile):
        up = dot_tn(o1_s[:, at : at + tile], gpre_s[...])
        for part in range(hidden // width):
            pack(base + part * width + at, up[:, part * width : (part + 1) * width])
    base = base + hidden
    for at in range(0, hidden, tile):
        pack(base + at, dot_tn(act_s[:, at : at + tile], gffn_s[...]))
    base = base + hidden
    pack(base, dot(normed_t[:, own], gbl_s[...]))
    base = base + columns
    pack(base, jnp.concatenate([small[:, :width], small[:, width:]], axis=0))
    base = base + 16
    if base < early_x.shape[1]:
        early_x[:, base:, :] = jnp.zeros((2, early_x.shape[1] - base, half), BF)
    early.stage(0)

    dq = att
    grad_normed = sbuf.at[0, 0:columns, :]
    moment = sbuf.at[0, columns : 2 * columns, 0 : 3 * width]
    mine = sbuf.at[1, 0:cols_mine, :]
    colsum = sbuf.at[1, cols_mine : cols_mine + 8, 0 : 3 * width]
    dq[...] = jnp.zeros(dq.shape, F32)
    moment[...] = jnp.zeros(moment.shape, F32)
    colsum[...] = jnp.zeros(colsum.shape, F32)
    dkv = act_s
    slots = SLOTS_AT[: min(len(SLOTS_AT), early.stages - 1)]

    @pl.loop(0, rows // k_step)
    def _(chunk):
        k_rows = pl.ds(pl.multiple_of(chunk * k_step, k_step), k_step)
        aug = key_aug[k_rows, :]
        for head in range(HEADS):
            lanes = slice(head * HD, (head + 1) * HD)
            q = query[:, lanes]
            k = keys[k_rows, lanes]
            do = grad_att[:, lanes]
            s = dot_nt(
                jnp.concatenate([k, aug], axis=1),
                jnp.concatenate([q, query_aug[head]], axis=1),
            )
            p = jnp.exp2(s)
            dp = dot_nt(
                jnp.concatenate([vals[k_rows, lanes], aug], axis=1),
                jnp.concatenate([do, att_aug[head]], axis=1),
            )
            ds = (p * dp).astype(BF)
            dv = dot(p.astype(BF), do)
            dk = dot(ds, q) * (1.0 / LOG2E)
            k_lanes = slice(head * HD, (head + 1) * HD)
            v_lanes = slice(width + head * HD, width + (head + 1) * HD)
            dkv[0:k_step, k_lanes] = dk.astype(BF)
            dkv[0:k_step, v_lanes] = dv.astype(BF)
            for part, value in ((1, dk), (2, dv)):
                lo = part * width + head * HD
                colsum[0:1, lo : lo + HD] += jnp.sum(value, axis=0, keepdims=True)
            dq[:, lanes] += dot_tn(ds, k)
            if head % 2 == 1:
                for number, when in enumerate(slots):

                    @pl.when(2 * chunk + head // 2 == when)
                    def _(number=number):
                        early.stage(number + 1)

        grads = dkv[0:k_step, :]
        moment[:, width:] += dot(normed_t[:, k_rows], grads)
        grad_normed[:, k_rows] = dot_nt(w_pair[0:columns, width:], grads)

    dql = (dq[...] * (1.0 / math.sqrt(HD))).astype(BF)
    colsum[0:1, 0:width] = jnp.sum(dql.astype(F32), axis=0, keepdims=True)
    moment[:, 0:width] = dot(normed_t[:, own], dql)
    grad_normed[:, own] += dot_nt(w_pair[0:columns, 0:width], dql) + dot_nt(w_enc[...], gbl_s[...])
    for i in range(feat_count):
        grad_low[i] = grad_normed[i * cols_mine : (i + 1) * cols_mine, :].astype(BF)

    order = bits_below(feat_count)
    index, number = {}, 0
    for bit in order:
        for i in range(feat_count // (2 * bit)):
            index[bit, i] = number
            number += 1

    def copy(bit, i):
        j = 1 - bit_of(me, bit) + 2 * i
        src = grad_low.at[j] if bit == 1 else held.at[index[bit // 2, 0] + j]
        return send(
            src, grad_in.at[index[bit, i]], (rsend, rrecv), index[bit, i],
            {"feat": flip(me, bit)},
        )

    start_all([copy(1, i) for i in range(feat_count // 2)])
    late_x[...] = jnp.zeros(late_x.shape, BF)
    for part in range(3):
        for side in range(2):
            lanes = slice(part * width + side * half, part * width + (side + 1) * half)
            late_x[side, part * columns : (part + 1) * columns, :] = moment[:, lanes].astype(BF)
            at = 3 * columns + 16 * part
            late_x[side, at : at + 16, :] = jnp.concatenate(
                [colsum[:, lanes], jnp.zeros((8, half), F32)], axis=0
            ).astype(BF)
    late.stage(0)
    for level, bit in enumerate(order):
        for i in range(feat_count // (2 * bit)):
            copy(bit, i).wait()
            j = bit_of(me, bit) + 2 * i
            here = grad_low[j] if bit == 1 else held[index[bit // 2, 0] + j]
            total = here.astype(F32) + grad_in[index[bit, i]].astype(F32)
            if level + 1 < len(order):
                held[index[bit, i]] = total.astype(BF)
            else:
                mine[...] = total
        if level + 1 < len(order):
            start_all([copy(2 * bit, i) for i in range(feat_count // (4 * bit))])
        if level == 0:
            late.stage(1)
    for number in range(len(slots) + 1, early.stages):
        early.stage(number)
    store_early = pltpu.make_async_copy(early_o, early_h, local_sem.at[8])
    store_early.start()

    def gather(v, member):
        high, mid, small = split3(v)
        return dot_nt(high, member) + dot_nt(mid, member) + dot_nt(small, member)

    d_factor = jnp.zeros((cols_mine, SLOTS), F32)
    for cut in pieces:
        d_factor = d_factor + gather(mine[:, cut] * cent[:, cut], mem_t[:, cut])
    late.stage(2)
    side = jnp.where(var > 0.25, 1.0, jnp.where(var == 0.25, 0.5, 0.0))
    d_var = d_factor * (-0.5) * factor / jnp.maximum(var, 0.25) * side
    pull = 2.0 * d_var / count
    d_mean = jnp.zeros((cols_mine, SLOTS), F32)
    for cut in pieces:
        dc = mine[:, cut] * dot_split(factor, mem_t[:, cut]) + cent[:, cut] * dot_split(
            pull, tr_t[:, cut]
        )
        grad_x[:, cut] = dc
        d_mean = d_mean - gather(dc, mem_t[:, cut])
    d_mean = d_mean / count
    for cut in pieces:
        grad_x[:, cut] = grad_x[:, cut] + dot_split(d_mean, tr_t[:, cut])
    for number in range(3, late.stages):
        late.stage(number)
    store_out.wait()
    store_early.wait()


def finish_kernel(
    early, late, w_enc, w_qkv, b_enc,
    g_w_enc, g_b_enc, g_w_qkv, g_b_query, g_b_value, g_w_out, g_b_out, g_gain_one,
    g_shift_one, g_w_up, g_b_up, g_w_down, g_b_down, g_gain_two, g_shift_two,
    moment_s, sums_s, *, places,
):
    columns, width = w_enc.shape
    hidden = g_w_up.shape[1]
    half = width // 2
    cols_mine = g_w_enc.shape[0]

    def take(ref, lo, count):
        return jnp.concatenate([ref[0, lo : lo + count, :], ref[1, lo : lo + count, :]], axis=1)

    step = 256
    for lo in range(0, width, step):
        g_w_out[lo : lo + step, :] = take(early, lo, step).astype(F32)
    base = width
    for part in range(hidden // width):
        for lo in range(0, width, step):
            g_w_up[lo : lo + step, part * width : (part + 1) * width] = take(
                early, base + part * width + lo, step
            ).astype(F32)
    base = base + hidden
    for lo in range(0, hidden, step):
        g_w_down[lo : lo + step, :] = take(early, base + lo, step).astype(F32)
    base = base + hidden
    for part in range(3):
        moment_s[:, part * width : (part + 1) * width] = take(late, part * columns, columns)
        sums_s[:, part * width : (part + 1) * width] = take(
            late, 3 * columns + 16 * part, 16
        )
    sums = sums_s[0:1, :].astype(F32)
    b_high, b_mid, b_low = split3(b_enc[...])
    for lo in range(0, 3 * width, width):
        cut = slice(lo, lo + width)
        s = sums_s[0:1, cut]
        outer = dot_tn(b_high, s) + dot_tn(b_mid, s) + dot_tn(b_low, s)
        g_w_qkv[:, cut] = dot_tn(w_enc[...], moment_s[:, cut]) + outer
    me = lax.axis_index("feat")
    own = pl.ds(pl.multiple_of(me * cols_mine, cols_mine), cols_mine)
    own_local = pl.ds(pl.multiple_of(base + me * cols_mine, cols_mine), cols_mine)
    local = jnp.concatenate([early[0, own_local, :], early[1, own_local, :]], axis=1)
    g_w_enc[...] = dot_nt(moment_s[own, :], w_qkv[...]) + local.astype(F32)
    small = take(early, base + columns, 16).astype(F32)
    g_b_enc[...] = dot_nt(sums_s[...], w_qkv[...])[0:1, :] + small[6:7, :]
    g_b_query[...] = sums[:, :width]
    g_b_value[...] = sums[:, 2 * width :]
    g_b_out[...] = small[6:7, :]
    g_gain_one[...] = small[4:5, :]
    g_shift_one[...] = small[5:6, :]
    g_b_up[...] = jnp.concatenate([small[3:4, :], small[11:12, :]], axis=1)
    g_b_down[...] = small[2:3, :]
    g_gain_two[...] = small[0:1, :]
    g_shift_two[...] = small[1:2, :]


def spec(kind):
    return pl.BlockSpec(memory_space={"v": pltpu.VMEM, "s": pltpu.SMEM, "h": pl.ANY}[kind])


def call(kernel, ins, args, outs, scratch, **params):
    return pl.pallas_call(
        kernel,
        out_shape=tuple(jax.ShapeDtypeStruct(shape, kind) for _, shape, kind in outs),
        in_specs=[spec(k) for k in ins],
        out_specs=tuple(spec(k) for k, _, _ in outs),
        scratch_shapes=[
            pltpu.SemaphoreType.DMA((entry,)) if isinstance(entry, int) else pltpu.VMEM(*entry)
            for entry in scratch
        ],
        compiler_params=pltpu.CompilerParams(vmem_limit_bytes=VMEM_BYTES, **params),
    )(*args)


def per_device(
    features, lengths, train_counts, used_features, w_enc, b_enc, w_qkv, b_query, b_value,
    w_out, b_out, gain_one, shift_one, w_up, b_up, w_down, b_down, gain_two, shift_two, cotangent,
):
    places = {"feat": lax.axis_size("feat"), "rows": lax.axis_size("rows")}
    feat_count = places["feat"]
    rows, cols_mine = features.shape
    columns = cols_mine * feat_count
    width = w_qkv.shape[0]
    hidden = w_up.shape[1]
    rows_mine = rows // feat_count
    half = width // 2
    early_group, late_group = 2, 4
    early_rows, early_parts, early_sems, early_land = reduce_plan(
        width + 2 * hidden + columns + 16, places, early_group
    )
    late_rows, late_parts, late_sems, late_land = reduce_plan(
        3 * columns + 48, places, late_group
    )
    row = lambda v: v.reshape(1, -1)
    gather_sems = 5 * (feat_count - 1)
    out, early, late, grad_x, w_enc_all = call(
        functools.partial(
            layer_kernel, places=places, early_parts=early_parts, early_group=early_group,
            late_parts=late_parts, late_group=late_group,
        ),
        "sss" + "v" * 12 + "h" * 5,
        (
            lengths, train_counts, used_features, features.T, w_enc, row(b_enc), row(b_query),
            row(b_value), row(b_out), row(gain_one), row(shift_one), row(b_up), row(b_down),
            row(gain_two), row(shift_two), w_qkv, w_out, w_up, w_down, cotangent,
        ),
        [
            ("h", (rows_mine, width), BF), ("h", (2, early_rows, half), BF),
            ("v", (2, late_rows, half), BF), ("v", (cols_mine, rows), F32),
            ("v", (columns, width), BF),
        ],
        [
            (w_out.shape, BF), (w_up.shape, BF), (w_down.shape, BF),
            ((rows_mine, width), BF),
            ((SLOTS, rows), BF), ((SLOTS, rows), BF), ((8, SLOTS), F32), ((rows, HD), BF),
            ((cols_mine, rows), F32), ((columns, rows), BF), ((2 * columns, 3 * width), BF),
            ((rows, width), BF), ((rows, width), BF), ((rows_mine, width), BF),
            ((rows_mine, width), F32), ((rows_mine, width), F32),
            ((HEADS, rows_mine, HD), BF), ((rows_mine, width), BF), ((HEADS, rows_mine, HD), BF),
            ((2, min(256, rows_mine), rows), F32),
            ((8, hidden), F32), ((rows_mine, width), BF), ((rows_mine, width), BF),
            ((rows_mine, width), BF), ((rows_mine, width), BF), ((rows_mine, hidden), BF),
            ((rows_mine, hidden), BF),
            ((2, early_rows, half), BF), ((2, early_rows, half), BF), ((early_rows, half), BF),
            ((early_land, half), BF), ((feat_count, cols_mine, rows), BF),
            ((2, late_rows, half), BF), ((late_rows, half), BF), ((late_land, half), BF),
            ((feat_count - 1, cols_mine, rows), BF), ((feat_count - 1, cols_mine, rows), BF),
            9, gather_sems, gather_sems, early_sems, early_sems, late_sems, late_sems,
            feat_count - 1, feat_count - 1,
        ],
        collective_id=0, has_side_effects=True,
    )
    vector = ("v", (1, width), F32)
    grads = call(
        functools.partial(finish_kernel, places=places),
        "v" * 5,
        (early, late, w_enc_all, w_qkv, row(b_enc)),
        [
            ("v", (cols_mine, width), F32), vector,
            ("v", (width, 3 * width), F32), vector, vector, ("v", (width, width), F32), vector,
            vector, vector, ("v", (width, hidden), F32), ("v", (1, hidden), F32),
            ("v", (hidden, width), F32), vector, vector, vector,
        ],
        [((columns, 3 * width), BF), ((16, 3 * width), BF)],
    )
    return (out, grad_x.T) + tuple(g.reshape(-1) if g.shape[0] == 1 else g for g in grads)


def solution(mesh):
    whole = P()
    in_specs = (
        (P("rows", "feat"),) + (P("rows", None),) * 3 + (P("feat", None),) + (whole,) * 14
        + (P(("rows", "feat"), None),)
    )
    out_specs = (
        (P(("rows", "feat"), None), P("rows", "feat"), P("feat", None)) + (whole,) * 14
    )
    return jax.shard_map(
        per_device, mesh=mesh, in_specs=in_specs, out_specs=out_specs, check_vma=False
    )
```

```python
import functools
import math

import jax
import jax.numpy as jnp
from jax import lax
from jax.experimental import pallas as pl
from jax.experimental.pallas import tpu as pltpu
from jax.sharding import PartitionSpec as P

HEADS = 4
HD = 128
FEATS = 100
EPS = 1e-5
LOG2E = 1.4426950408889634
BIG = 1e30
SLOTS = 8
PASSES = 2
EARLY_AT = (0, 4, 7, 10)
LATE_AT = (1, 6)
VMEM_BYTES = 63 * 1024 * 1024

BF = jnp.bfloat16
F32 = jnp.float32
MESH = pl.DeviceIdType.MESH


def dot(a, b):
    return lax.dot_general(a, b, (((1,), (0,)), ((), ())), preferred_element_type=F32)


def dot_nt(a, b):
    return lax.dot_general(a, b, (((1,), (1,)), ((), ())), preferred_element_type=F32)


def dot_tn(a, b):
    return lax.dot_general(a, b, (((0,), (0,)), ((), ())), preferred_element_type=F32)


def split3(v):
    high = v.astype(BF)
    rest = v - high.astype(F32)
    mid = rest.astype(BF)
    return high, mid, (rest - mid.astype(F32)).astype(BF)


def dot_split(v, b):
    high, mid, small = split3(v)
    return dot(high, b) + dot(mid, b) + dot(small, b)


def aug_lanes(base, value):
    high, mid, small = (part.astype(F32) for part in split3(value))
    lane = lax.broadcasted_iota(jnp.int32, base.shape, 1)
    out = jnp.where(lane == SLOTS, high, base.astype(F32))
    out = jnp.where(lane == SLOTS + 1, mid, out)
    return jnp.where(lane == SLOTS + 2, small, out).astype(BF)

def bits_below(count):
    return [1 << i for i in range(count.bit_length() - 1)]


def bit_of(index, bit):
    return lax.rem(index // bit, 2)


def flip(index, bit):
    return index + bit * (1 - 2 * bit_of(index, bit))


def greet(peers):
    barrier = pltpu.get_barrier_semaphore()
    for peer in peers:
        pl.semaphore_signal(barrier, inc=1, device_id=peer, device_id_type=MESH)


def await_greetings(peers):
    pl.semaphore_wait(pltpu.get_barrier_semaphore(), len(peers))


def send(src, dst, sems, slot, peer):
    return pltpu.make_async_remote_copy(
        src_ref=src, dst_ref=dst, send_sem=sems[0].at[slot], recv_sem=sems[1].at[slot],
        device_id=peer, device_id_type=MESH,
    )


def gather_steps(feat_count):
    steps, held = [], [()]
    for bit in bits_below(feat_count)[::-1]:
        steps += [(path, bit) for path in held]
        held = held + [path + (bit,) for path in held]
    return steps


def feat_others(me, feat_count):
    bits = bits_below(feat_count)
    subsets = sorted(range(1, feat_count), key=lambda subset: bin(subset).count("1"))
    found = []
    for subset in subsets:
        at = me
        for bit in bits:
            if subset & bit:
                at = flip(at, bit)
        found.append(at)
    return found


class GatherFeat:
    def __init__(self, full, block, piece, sems, first, feat_count):
        self.full, self.block, self.piece = full, block, piece
        self.sems, self.first = sems, first
        self.steps = gather_steps(feat_count)
        self.me = lax.axis_index("feat")
        self.waited = set()

    def copy(self, number, at):
        path, bit = self.steps[number]
        index = self.me
        for done in path:
            index = flip(index, done)
        part = self.full.at[
            pl.ds(pl.multiple_of(index * self.block, self.block), self.block),
            pl.ds(at * self.piece, self.piece),
        ]
        slot = self.first + at * len(self.steps) + number
        return send(part, part, self.sems, slot, {"feat": flip(self.me, bit)})

    def arrived(self, number, at):
        if (number, at) not in self.waited:
            self.waited.add((number, at))
            self.copy(number, at).wait_recv()

    def start(self, at):
        for number, (path, _) in enumerate(self.steps):
            if not path:
                self.copy(number, at).start()

    def forward(self, at):
        for number, (path, _) in enumerate(self.steps):
            if path:
                self.arrived(self.steps.index((path[:-1], path[-1])), at)
                self.copy(number, at).start()

    def finish(self, at):
        for number in range(len(self.steps)):
            self.arrived(number, at)
        for number in range(len(self.steps)):
            self.copy(number, at).wait_send()


def chunked(items, size):
    return [items[i : i + size] for i in range(0, len(items), size)]


class AllReduce:
    def __init__(self, x, out, first_in, later_in, sems, places, parts, group, sem=0):
        self.x, self.out, self.sem, self.size = x, out, sem, sum(parts)
        self.first_in, self.later_in, self.sems = first_in, later_in, sems
        self.place = {axis: lax.axis_index(axis) for axis in places}
        self.core = bit_of(self.place["feat"], 1)
        groups = chunked(reduce_bits(places), group)
        self.depth = len(groups)
        self.parts = []
        self.count = sem + 2
        start = 0
        for number, size in enumerate(parts):
            turn = number * len(groups) // len(parts)
            at, landing, levels = start, start, []
            length = size
            for bits in groups[turn:] + groups[:turn]:
                length = length // 2 ** len(bits)
                member = sum(self.bit(b) << i for i, b in enumerate(bits))
                peers = []
                for subset in range(1, 2 ** len(bits)):
                    theirs = member
                    where = dict(self.place)
                    for i, (axis, bit) in enumerate(bits):
                        if subset >> i & 1:
                            theirs = theirs + (1 - 2 * self.bit((axis, bit))) * 2**i
                            where[axis] = flip(where[axis], bit)
                    peers.append((where, at + theirs * length, landing, self.count))
                    landing += length
                    self.count += 2
                at = at + member * length
                levels.append((peers, at, length))
            self.parts.append(levels)
            start += size

    def bit(self, which):
        return bit_of(self.place[which[0]], which[1])

    def rows(self, which, side, at, size):
        ref, base = which
        return ref.at[pl.ds(pl.multiple_of(base + side * self.size + at, 16), size)]

    def core_in(self):
        return send(
            self.rows(self.x, 1 - self.core, 0, self.size), self.first_in, self.sems, self.sem,
            self.peers()[0],
        )

    def core_out(self):
        half = self.rows(self.out, self.core, 0, self.size)
        return send(half, half, self.sems, self.sem + 1, self.peers()[0])

    def down(self, part, level):
        peers, _, size = self.parts[part][level]
        return [
            send(
                self.rows(self.x, self.core, at, size), self.later_in.at[pl.ds(landing, size)],
                self.sems, slot, where,
            )
            for where, at, landing, slot in peers
        ]

    def up(self, part, level):
        peers, at, size = self.parts[part][level]
        seg = self.rows(self.out, self.core, at, size)
        return [send(seg, seg, self.sems, slot + 1, where) for where, _, _, slot in peers]

    def stage(self, number):
        depth = self.depth
        everyone = range(len(self.parts))
        if number == 0:
            self.core_in().start()
        elif number == 1:
            self.core_in().wait()
            mine = self.rows(self.x, self.core, 0, self.size)
            mine[...] = (mine[...].astype(F32) + self.first_in[...].astype(F32)).astype(BF)
            for part in everyone:
                start_all(self.down(part, 0))
        elif number <= depth + 1:
            level = number - 2
            for part in everyone:
                wait_all(self.down(part, level))
                peers, at, size = self.parts[part][level]
                mine = self.rows(self.x, self.core, at, size)
                total = mine[...].astype(F32)
                for _, _, landing, _ in peers:
                    total = total + self.later_in[landing : landing + size, :].astype(F32)
                if level + 1 < depth:
                    mine[...] = total.astype(BF)
                    start_all(self.down(part, level + 1))
                else:
                    self.rows(self.out, self.core, at, size)[...] = total.astype(BF)
                    start_all(self.up(part, level))
        elif number <= 2 * depth + 1:
            level = depth - 1 - (number - depth - 2)
            for part in everyone:
                wait_all(self.up(part, level))
                if level > 0:
                    start_all(self.up(part, level - 1))
            if level == 0:
                self.core_out().start()
        else:
            self.core_out().wait()

    @property
    def stages(self):
        return 2 * self.depth + 3

    def peers(self):
        first = dict(self.place)
        first["feat"] = flip(first["feat"], 1)
        return [first] + [where for peers, _, _ in self.parts[0] for where, _, _, _ in peers]


def start_all(copies):
    for copy in copies:
        copy.start()


def wait_all(copies):
    for copy in copies:
        copy.wait()


def reduce_bits(places):
    return [("feat", b) for b in bits_below(places["feat"])[1:]] + [
        ("rows", b) for b in bits_below(places["rows"])
    ]


def reduce_plan(rows_needed, places, group):
    bits = reduce_bits(places)
    groups = chunked(bits, group)
    granule = 16 * 2 ** len(bits)
    units = -(-rows_needed // granule)
    first = -(-units * 2 // 3)
    parts = [first, units - first] if len(groups) > 1 and units > 1 else [units]
    parts = [size * granule for size in parts]
    sems = 2 + 2 * len(parts) * sum(2 ** len(g) - 1 for g in groups)
    landing = sum(parts)
    return sum(parts), parts, sems, landing


def tile_lanes(v, wide):
    return jnp.concatenate([v] * (wide // v.shape[1]), axis=1)


def table_masks(refs, mem_t, tr_t, tab):
    lengths, trains, used = refs
    tables = lengths.shape[1]
    slots, rows = mem_t.shape
    row = lax.broadcasted_iota(jnp.int32, (slots, rows), 0)
    at = lax.broadcasted_iota(jnp.int32, (slots, rows), 1)
    slot = lax.broadcasted_iota(jnp.int32, (8, slots), 1)
    line = lax.broadcasted_iota(jnp.int32, (8, slots), 0)
    member = jnp.zeros((slots, rows), jnp.bool_)
    train = jnp.zeros((slots, rows), jnp.bool_)
    counts = jnp.where(line < 2, 1, 0)
    start = jnp.int32(0)
    for j in range(tables):
        stop = start + lengths[0, j]
        learned = start + trains[0, j]
        here = (row == j) & (at >= start)
        member = member | (here & (at < stop))
        train = train | (here & (at < learned))
        counts = jnp.where((slot == j) & (line == 0), trains[0, j], counts)
        counts = jnp.where((slot == j) & (line > 0), used[0, j], counts)
        start = stop
    mem_t[...] = jnp.where(member, 1.0, 0.0).astype(BF)
    tr_t[...] = jnp.where(train, 1.0, 0.0).astype(BF)
    counts = counts.astype(F32)
    tab[...] = jnp.where(line == 1, jnp.sqrt(FEATS / jnp.maximum(counts, 1.0)), counts)


def key_masks(refs, key_aug):
    lengths, trains = refs
    lane = lax.broadcasted_iota(jnp.int32, (1, HD), 1)
    rows = key_aug.shape[0]
    low = jnp.full((1, HD), rows, jnp.int32)
    high = jnp.full((1, HD), 0, jnp.int32)
    start = jnp.int32(0)
    for j in range(lengths.shape[1]):
        low = jnp.where(lane == j, start, low)
        high = jnp.where(lane == j, start + trains[0, j], high)
        start = start + lengths[0, j]
    step = 512

    @pl.loop(0, rows // step)
    def _(block):
        token = lax.broadcasted_iota(jnp.int32, (step, HD), 0) + block * step
        wide = lax.broadcasted_iota(jnp.int32, (step, HD), 1)
        open_to = (token >= low) & (token < high)
        mask = jnp.where(wide < SLOTS, jnp.where(open_to, 0.0, -BIG), 0.0)
        ones = (wide >= SLOTS) & (wide < SLOTS + 3)
        key_aug[pl.ds(pl.multiple_of(block * step, step), step), :] = jnp.where(
            ones, 1.0, mask
        ).astype(BF)


def layer_kernel(
    lengths, trains, used, features_t, w_mine, b_enc, b_query, b_value, b_out, gain_one, shift_one,
    b_up, b_down, gain_two, shift_two,
    w_qkv_h, w_out_h, w_up_h, w_down_h, cot_h,
    out_h, early_h, late_h, grad_x, w_enc,
    w_out, w_up, w_down, cot,
    mem_t, tr_t, tab, key_aug, cent, normed_t, w_pair, keys, vals, query, enc, att,
    query_aug, grad_att, att_aug, sbuf,
    small, stash, early_x, first_e, later_e, grad_low,
    first_l, later_l, held, grad_in, own_low, own_in,
    local_sem, gsend, grecv, esend, erecv, lsend, lrecv, rsend, rrecv, osend, orecv,
    *, places, early_parts, early_group, late_parts, late_group,
):
    feat_count = places["feat"]
    me = lax.axis_index("feat")
    cols_mine, rows = features_t.shape
    columns, width = w_enc.shape
    hidden = w_up.shape[1]
    rows_mine = query.shape[0]
    row_lo = pl.multiple_of(me * rows_mine, rows_mine)
    col_lo = pl.multiple_of(me * cols_mine, cols_mine)
    half = width // 2

    taken = [0]

    def blocks(count):
        taken[0] += count
        return [
            stash.at[pl.ds(i * rows_mine, rows_mine)] for i in range(taken[0] - count, taken[0])
        ]

    wide_blocks, deep_blocks = width // half, hidden // half
    attl_s, gbl_s, o1_s, gffn_s = (blocks(wide_blocks) for _ in range(4))
    gpre_s, act_s = (blocks(deep_blocks) for _ in range(2))

    def fill(parts, at, value):
        for i, part in enumerate(parts):
            part[at, :] = value[:, i * half : (i + 1) * half]

    def read(parts):
        return jnp.concatenate([part[...] for part in parts], axis=1)

    early_size, late_size = sum(early_parts), sum(late_parts)
    late_x = [2 * early_size + turn * 4 * late_size for turn in range(PASSES)]
    late_o = [at + 2 * late_size for at in late_x]
    early = AllReduce(
        (early_x, 0), (stash, 0), first_e, later_e, (esend, erecv), places, early_parts, early_group
    )
    late_sems = lsend.shape[0] // PASSES
    lates = [
        AllReduce(
            (stash, late_x[turn]), (stash, late_o[turn]), first_l.at[turn], later_l.at[turn],
            (lsend, lrecv), places, late_parts, late_group, turn * late_sems,
        )
        for turn in range(PASSES)
    ]
    w_qkv = [
        [
            stash.at[pl.ds((part * wide_blocks + i) * width, width)]
            for i in range(wide_blocks)
        ]
        for part in range(3)
    ]
    loads = [
        pltpu.make_async_copy(src, dst, local_sem.at[i])
        for i, (src, dst) in enumerate(
            [
                (w_qkv_h.at[:, pl.ds(part * width + i * half, half)], block)
                for part, w_part in enumerate(w_qkv)
                for i, block in enumerate(w_part)
            ]
            + [(cot_h, cot), (w_out_h, w_out), (w_up_h, w_up), (w_down_h, w_down)]
        )
    ]
    start_all(loads)
    peers = lates[0].peers() + [{"feat": at} for at in feat_others(me, feat_count)[2:]]
    greet(peers)

    table_masks((lengths, trains, used), mem_t, tr_t, tab)
    step = 512
    pieces = [slice(at, at + step) for at in range(0, rows, step)]
    count = tab[0:1, :]
    mean = jnp.zeros((cols_mine, SLOTS), F32)
    for cut in pieces:
        mean = mean + dot_nt(features_t[:, cut], tr_t[:, cut])
    mean = mean / count
    var = jnp.zeros((cols_mine, SLOTS), F32)
    for cut in pieces:
        c = features_t[:, cut].astype(F32) - dot_split(mean, mem_t[:, cut])
        cent[:, cut] = c
        high, mid, _ = split3(c * c)
        var = var + (dot_nt(high, tr_t[:, cut]) + dot_nt(mid, tr_t[:, cut]))
    var = var / count
    column = (lax.broadcasted_iota(jnp.int32, (cols_mine, SLOTS), 0) + col_lo).astype(F32)
    is_last = (
        lax.broadcasted_iota(jnp.int32, (cols_mine, 1), 0) + col_lo == columns - 1
    )
    factor = jnp.where(
        column < tab[2:3, :], lax.rsqrt(jnp.maximum(var, 0.25)) * tab[1:2, :], 0.0
    )
    for cut in pieces:
        normed_t[pl.ds(col_lo, cols_mine), cut] = jnp.where(
            is_last, 1.0, cent[:, cut] * dot_split(factor, mem_t[:, cut])
        ).astype(BF)
    w_enc[pl.ds(col_lo, cols_mine), :] = w_mine[...]
    await_greetings(peers)
    steps = len(gather_steps(feat_count))
    gather_w = GatherFeat(w_enc, cols_mine, width, (gsend, grecv), 0, feat_count)
    gather_w.start(0)
    splits = 4
    piece = rows // splits
    gather_x = GatherFeat(normed_t, cols_mine, piece, (gsend, grecv), steps, feat_count)
    for at in range(splits):
        gather_x.start(at)

    key_masks((lengths, trains), key_aug)
    gather_w.forward(0)
    gather_w.finish(0)
    last = lax.broadcasted_iota(jnp.int32, (columns, 1), 0) == columns - 1
    w_enc[...] = jnp.where(last, 0.0, w_enc[...].astype(F32)).astype(BF)
    wait_all(loads[: 3 * wide_blocks])
    for part, w_part in enumerate(w_qkv):
        lanes = slice(part * width, (part + 1) * width)
        w_now = read(w_part)
        bias = dot_split(jnp.broadcast_to(b_enc[...], (8, width)), w_now)[0:1, :]
        if part != 1:
            bias = bias + (b_query if part == 0 else b_value)[...]
        high, mid, _ = split3(jnp.where(last, bias, dot(w_enc[...], w_now)))
        w_pair[0:columns, lanes] = high
        w_pair[columns:, lanes] = mid

    def project(at):
        for lo in range(at * piece, (at + 1) * piece, step):
            n = normed_t[:, lo : lo + step].astype(F32).T.astype(BF)
            both = jnp.concatenate([n, n], axis=1)
            keys[lo : lo + step, :] = dot(both, w_pair[:, width : 2 * width]).astype(BF)
            vals[lo : lo + step, :] = dot(both, w_pair[:, 2 * width :]).astype(BF)

    gather_x.forward(0)
    for at in range(splits):
        if at + 1 < splits:
            gather_x.forward(at + 1)
        gather_x.finish(at)
        project(at)
    block = min(256, rows_mine)
    scale = LOG2E / math.sqrt(HD)
    for lo in range(0, rows_mine, block):
        cols = pl.ds(pl.multiple_of(row_lo + lo, block), block)
        n = normed_t[:, cols].astype(F32).T.astype(BF)
        both = jnp.concatenate([n, n], axis=1)
        query[lo : lo + block, :] = (dot(both, w_pair[:, 0:width]) * scale).astype(BF)
        enc[lo : lo + block, :] = dot(n, w_enc[...]) + b_enc[...]

    q_step = min(256, rows_mine)
    k_step = 512
    ones = jnp.ones((k_step, HD), BF)

    @pl.loop(0, rows_mine // q_step)
    def _(number):
        lo = pl.multiple_of(number * q_step, q_step)
        q_rows = pl.ds(lo, q_step)
        cols = pl.ds(pl.multiple_of(row_lo + lo, q_step), q_step)
        table = jnp.concatenate(
            [mem_t[:, cols].astype(F32), jnp.zeros((HD - SLOTS, q_step), F32)], axis=0
        ).T.astype(BF)
        for head in range(HEADS):
            lanes = slice(head * HD, (head + 1) * HD)
            q = jnp.concatenate([query[q_rows, lanes], table], axis=1)
            peak = jnp.full((q_step, HD), -3e38, F32)
            for at in range(0, rows, k_step):
                k_rows = slice(at, at + k_step)
                k = jnp.concatenate([keys[k_rows, lanes], key_aug[k_rows, :]], axis=1)
                s = dot_nt(q, k)
                sbuf[head % 2, :, k_rows] = s
                for lo in range(0, k_step, HD):
                    peak = jnp.maximum(peak, s[:, lo : lo + HD])
            top = jnp.broadcast_to(jnp.max(peak, axis=1, keepdims=True), (q_step, HD))
            total = jnp.zeros((q_step, 2 * HD), F32)
            for at in range(0, rows, k_step):
                k_rows = slice(at, at + k_step)
                p = jnp.exp2(sbuf[head % 2, :, k_rows] - tile_lanes(top, k_step)).astype(BF)
                v = jnp.concatenate([vals[k_rows, lanes], ones], axis=1)
                total = total + dot(p, v)
            norm = total[:, HD:]
            att[q_rows, lanes] = total[:, :HD] / norm
            query_aug[head, q_rows, :] = aug_lanes(table, -(top + jnp.log2(norm)))

    wait_all(loads[3 * wide_blocks :])
    small[...] = jnp.zeros(small.shape, F32)

    def add_small(slot, value, wide):
        small[slot : slot + 1, 0:wide] += jnp.sum(value, axis=0, keepdims=True)

    def mean_of(v):
        return jnp.mean(v, axis=1, keepdims=True)

    for lo in range(0, rows_mine, block):
        at = slice(lo, lo + block)
        attended = att[at, :]
        attl = attended.astype(BF)
        fill(attl_s, at, attl)
        resid = enc[at, :] + dot(attl, w_out[...]) + b_out[...]
        ctr = resid - mean_of(resid)
        rstd1 = lax.rsqrt(mean_of(ctr * ctr) + EPS)
        n1 = ctr * rstd1
        o1 = n1 * gain_one[...] + shift_one[...]
        o1l = o1.astype(BF)
        fill(o1_s, at, o1l)
        pre = dot(o1l, w_up[...]) + b_up[...]
        cdf = 0.5 + 0.5 * lax.erf(pre * (1.0 / math.sqrt(2.0)))
        slope = cdf + pre * (jnp.exp(-0.5 * pre * pre) * (1.0 / math.sqrt(2.0 * math.pi)))
        actl = (pre * cdf).astype(BF)
        fill(act_s, at, actl)
        r2 = o1 + dot(actl, w_down[...]) + b_down[...]
        ctr2 = r2 - mean_of(r2)
        rstd2 = lax.rsqrt(mean_of(ctr2 * ctr2) + EPS)
        n2 = ctr2 * rstd2
        go = cot[at, :].astype(F32)
        cot[at, :] = (n2 * gain_two[...] + shift_two[...]).astype(BF)
        add_small(0, go * n2, width)
        add_small(1, go, width)
        dn = go * gain_two[...]
        g2 = rstd2 * (dn - mean_of(dn) - n2 * mean_of(dn * n2))
        gfl = g2.astype(BF)
        fill(gffn_s, at, gfl)
        add_small(2, g2, width)
        gpl = (dot_nt(gfl, w_down[...]) * slope).astype(BF)
        fill(gpre_s, at, gpl)
        add_small(3, gpl.astype(F32), hidden)
        g1 = dot_nt(gpl, w_up[...]) + g2
        add_small(4, g1 * n1, width)
        add_small(5, g1, width)
        dn1 = g1 * gain_one[...]
        gr = rstd1 * (dn1 - mean_of(dn1) - n1 * mean_of(dn1 * n1))
        add_small(6, gr, width)
        gbl = gr.astype(BF)
        fill(gbl_s, at, gbl)
        ga = dot_nt(gbl, w_out[...]).astype(BF)
        grad_att[at, :] = ga
        prod = ga.astype(F32) * attended
        zero = jnp.zeros((block, HD), BF)
        for head in range(HEADS):
            lanes = slice(head * HD, (head + 1) * HD)
            row_sum = jnp.sum(prod[:, lanes], axis=1, keepdims=True)
            att_aug[head, at, :] = aug_lanes(zero, jnp.broadcast_to(-row_sum, (block, HD)))

    store_out = pltpu.make_async_copy(cot, out_h, local_sem.at[3 * wide_blocks + 4])
    store_out.start()

    def pack(at, value):
        count = value.shape[0]
        early_x[at : at + count, :] = value[:, :half].astype(BF)
        early_x[early_size + at : early_size + at + count, :] = value[:, half:].astype(BF)

    own = pl.ds(row_lo, rows_mine)
    for i, part in enumerate(attl_s):
        pack(i * half, dot_tn(part[...], read(gbl_s)))
    base = width
    for i, part in enumerate(o1_s):
        up = dot_tn(part[...], read(gpre_s))
        for j in range(hidden // width):
            pack(base + j * width + i * half, up[:, j * width : (j + 1) * width])
    base = base + hidden
    for i, part in enumerate(act_s):
        pack(base + i * half, dot_tn(part[...], read(gffn_s)))
    base = base + hidden
    pack(base, dot(normed_t[:, own], read(gbl_s)))
    base = base + columns
    pack(base, jnp.concatenate([small[:, :width], small[:, width:]], axis=0))
    base = base + 16
    if base < early_size:
        pack(base, jnp.zeros((early_size - base, width), F32))
    early.stage(0)

    wide = HEADS // PASSES * HD
    grad_normed = sbuf.at[0, 0:columns, :]
    moment = sbuf.at[0, columns : 2 * columns, 0 : 3 * wide]
    mine = sbuf.at[1, 0:cols_mine, :]
    grad_own = sbuf.at[1, cols_mine : cols_mine + columns, 0:rows_mine]
    w_low = w_pair.at[0:columns, :]
    grad_own[...] = dot_nt(w_enc[...], read(gbl_s))
    chunks = rows // k_step
    plan = {}

    def place(when, stage):
        plan.setdefault(min(when, chunks * PASSES), []).append(stage)

    for number in range(1, early.stages):
        when = EARLY_AT[number - 1] if number <= len(EARLY_AT) else 16
        place(when * chunks * PASSES // 16, functools.partial(early.stage, number))
    for turn in range(PASSES - 1):
        for number in range(1, lates[turn].stages):
            when = LATE_AT[number - 1] if number <= len(LATE_AT) else 16
            place((turn + 1) * chunks + when * chunks // 8,
                  functools.partial(lates[turn].stage, number))

    order = bits_below(feat_count)
    index = {}
    for bit in order:
        for i in range(feat_count // (2 * bit)):
            index[bit, i] = len(index)

    def piece_at(number):
        return pl.ds(pl.multiple_of(number * k_step, k_step), k_step)

    def copy(bit, i, number):
        j = 1 - bit_of(me, bit) + 2 * i
        src = grad_low if bit == 1 else held
        at = j if bit == 1 else index[bit // 2, 0] + j
        return send(
            src.at[at, :, piece_at(number)], grad_in.at[index[bit, i], :, piece_at(number)],
            (rsend, rrecv), index[bit, i] * chunks + number, {"feat": flip(me, bit)},
        )

    def sum_start(level, number):
        bit = order[level]
        start_all([copy(bit, i, number) for i in range(feat_count // (2 * bit))])

    def sum_step(level, number):
        bit = order[level]
        cut = piece_at(number)
        for i in range(feat_count // (2 * bit)):
            copy(bit, i, number).wait()
            j = bit_of(me, bit) + 2 * i
            here = grad_low[j, :, cut] if bit == 1 else held[index[bit // 2, 0] + j, :, cut]
            total = here.astype(F32) + grad_in[index[bit, i], :, cut].astype(F32)
            if level + 1 < len(order):
                held[index[bit, i], :, cut] = total.astype(BF)
            else:
                mine[:, cut] = total
        if level + 1 < len(order):
            sum_start(level + 1, number)

    for turn in range(PASSES):
        heads = range(turn * HEADS // PASSES, (turn + 1) * HEADS // PASSES)
        at_pass = slice(turn * wide, (turn + 1) * wide)
        dq = att.at[:, at_pass]
        dq[...] = jnp.zeros((rows_mine, wide), F32)
        moment[...] = jnp.zeros(moment.shape, F32)
        w_kv = jnp.concatenate(
            [w_low[:, part * width + turn * wide : part * width + (turn + 1) * wide]
             for part in (1, 2)],
            axis=1,
        )

        @pl.loop(0, chunks)
        def _(number, turn=turn, heads=heads, dq=dq, w_kv=w_kv):
            k_rows = piece_at(number)
            aug = key_aug[k_rows, :]
            dks, dvs = [], []
            for head in heads:
                lanes = slice(head * HD, (head + 1) * HD)
                q = query[:, lanes]
                k = keys[k_rows, lanes]
                do = grad_att[:, lanes]
                s = dot_nt(
                    jnp.concatenate([k, aug], axis=1),
                    jnp.concatenate([q, query_aug[head]], axis=1),
                )
                p = jnp.exp2(s)
                dp = dot_nt(
                    jnp.concatenate([vals[k_rows, lanes], aug], axis=1),
                    jnp.concatenate([do, att_aug[head]], axis=1),
                )
                ds = (p * dp).astype(BF)
                dvs.append(dot(p.astype(BF), do).astype(BF))
                dks.append((dot(ds, q) * (1.0 / LOG2E)).astype(BF))
                into = slice((head - heads[0]) * HD, (head - heads[0] + 1) * HD)
                dq[:, into] += dot_tn(ds, k)
            grads = jnp.concatenate(dks + dvs, axis=1)
            moment[:, wide:] += dot(normed_t[:, k_rows], grads)
            product = dot_nt(w_kv, grads)
            if turn > 0:
                product = product + grad_normed[:, k_rows]
            if turn + 1 < PASSES:
                grad_normed[:, k_rows] = product
            else:
                for i in range(feat_count):
                    grad_low[i, :, k_rows] = product[i * cols_mine : (i + 1) * cols_mine, :].astype(
                        BF
                    )
                sum_start(0, number)

                @pl.when(number > 0)
                def _():
                    sum_step(0, number - 1)

            for when, stages in plan.items():
                if turn * chunks <= when < (turn + 1) * chunks:

                    @pl.when(number == when - turn * chunks)
                    def _(stages=stages):
                        for stage in stages:
                            stage()

        dql = (dq[...] * (1.0 / math.sqrt(HD))).astype(BF)
        moment[:, 0:wide] = dot(normed_t[:, own], dql)
        parts = jnp.concatenate(
            [moment[:, part * wide : (part + 1) * wide].astype(BF) for part in range(3)], axis=0
        )
        both = parts.shape[0] // 2
        for side in range(2):
            at = late_x[turn] + side * late_size
            stash[at : at + both, :] = parts[side * both : (side + 1) * both, :]
            if both < late_size:
                stash[at + both : at + late_size, :] = jnp.zeros((late_size - both, half), BF)
        lates[turn].stage(0)
        grad_own[...] += dot_nt(w_low[:, at_pass], dql)

    for i in range(feat_count):
        own_low[i] = grad_own[i * cols_mine : (i + 1) * cols_mine, :].astype(BF)
    swaps = []
    for number, other in enumerate(feat_others(me, feat_count)):
        swaps.append(
            send(own_low.at[other], own_in.at[me], (osend, orecv), number, {"feat": other})
        )
    start_all(swaps)
    own_in[me] = own_low[me]
    left = plan.get(chunks * PASSES, [])
    late = lates[-1]
    late.stage(1)
    sum_step(0, chunks - 1)
    for stage in left[:1]:
        stage()
    for level in range(1, len(order)):
        for number in range(chunks):
            sum_step(level, number)
    late.stage(2)
    wait_all(swaps)
    for i in range(feat_count):
        span = slice(i * rows_mine, (i + 1) * rows_mine)
        mine[:, span] += own_in[i].astype(F32)

    def gather(v, member):
        high, mid, small = split3(v)
        return dot_nt(high, member) + dot_nt(mid, member) + dot_nt(small, member)

    d_factor = jnp.zeros((cols_mine, SLOTS), F32)
    for cut in pieces:
        d_factor = d_factor + gather(mine[:, cut] * cent[:, cut], mem_t[:, cut])
    side = jnp.where(var > 0.25, 1.0, jnp.where(var == 0.25, 0.5, 0.0))
    d_var = d_factor * (-0.5) * factor / jnp.maximum(var, 0.25) * side
    pull = 2.0 * d_var / count
    d_mean = jnp.zeros((cols_mine, SLOTS), F32)
    for cut in pieces:
        dc = mine[:, cut] * dot_split(factor, mem_t[:, cut]) + cent[:, cut] * dot_split(
            pull, tr_t[:, cut]
        )
        grad_x[:, cut] = dc
        d_mean = d_mean - gather(dc, mem_t[:, cut])
    d_mean = d_mean / count
    for cut in pieces:
        grad_x[:, cut] = grad_x[:, cut] + dot_split(d_mean, tr_t[:, cut])
    for number in range(3, late.stages - 1):
        late.stage(number)
    for stage in left[1:]:
        stage()
    stores = [
        pltpu.make_async_copy(
            stash.at[pl.ds(at, count)], into, local_sem.at[3 * wide_blocks + 5 + i]
        )
        for i, (at, count, into) in enumerate(
            [(0, 2 * early_size, early_h)]
            + [
                (late_o[turn], 2 * late_size, late_h.at[pl.ds(turn * 2 * late_size, 2 * late_size)])
                for turn in range(PASSES)
            ]
        )
    ]
    start_all(stores[:-1])
    late.stage(late.stages - 1)
    stores[-1].start()
    store_out.wait()
    wait_all(stores)


def finish_kernel(
    early_h, late, w_enc, w_qkv_h, b_enc, out_in, grad_x_in,
    out, grad_x, g_w_enc, g_b_enc, g_w_qkv_h, g_b_query, g_b_value, g_w_out_h, g_b_out,
    g_gain_one, g_shift_one, g_w_up_h, g_b_up, g_w_down_h, g_b_down, g_gain_two, g_shift_two,
    early, w_qkv, g_w_qkv, g_w_out, g_w_up, g_w_down, moment_s, out_s, grad_x_s, sem,
):
    columns, width = w_enc.shape
    hidden = g_w_up.shape[1]
    cols_mine = g_w_enc.shape[0]
    places = [0]

    def copy(src, dst):
        places[0] += 1
        made = pltpu.make_async_copy(src, dst, sem.at[places[0] - 1])
        made.start()
        return made

    rest = width + 2 * hidden
    size = early.shape[0] // 2
    cuts = [
        pl.ds(rest, size - rest), pl.ds(0, width), pl.ds(width, hidden),
        pl.ds(width + hidden, hidden),
    ]
    loads = [
        [
            copy(
                early_h.at[pl.ds(side * size + cut.start, cut.size)],
                early.at[pl.ds(side * size + cut.start, cut.size)],
            )
            for side in range(2)
        ]
        for cut in cuts
    ]
    load_w = copy(w_qkv_h, w_qkv)
    passing = [copy(out_in, out_s), copy(grad_x_in, grad_x_s)]
    pending = []

    late_size = late.shape[0] // (2 * PASSES)
    wide = width // PASSES
    for turn in range(PASSES):
        starts = [(2 * turn + side) * late_size for side in range(2)]
        rows = jnp.concatenate([late[at : at + 3 * columns // 2, :] for at in starts], axis=0)
        for part in range(3):
            lo = part * width + turn * wide
            moment_s[:, lo : lo + wide] = rows[part * columns : (part + 1) * columns, :]
    bias = split3(b_enc[...])
    for lo in range(0, 3 * width, width):
        cut = slice(lo, lo + width)
        sums = moment_s[columns - 1 : columns, cut]
        outer = dot_tn(bias[0], sums) + dot_tn(bias[1], sums) + dot_tn(bias[2], sums)
        g_w_qkv[:, cut] = dot_tn(w_enc[...], moment_s[:, cut]) + outer
        lanes = pl.ds(lo, width)
        pending.append(copy(g_w_qkv.at[:, lanes], g_w_qkv_h.at[:, lanes]))

    wait_all(passing)
    pending += [copy(out_s, out), copy(grad_x_s, grad_x)]

    def take(lo, count):
        return jnp.concatenate(
            [early[lo : lo + count, :], early[size + lo : size + lo + count, :]], axis=1
        )

    step = 256
    wait_all(loads[1])
    for lo in range(0, width, step):
        g_w_out[lo : lo + step, :] = take(lo, step).astype(F32)
    pending.append(copy(g_w_out, g_w_out_h))
    wait_all(loads[2])
    for part in range(hidden // width):
        for lo in range(0, width, step):
            g_w_up[lo : lo + step, part * width : (part + 1) * width] = take(
                width + part * width + lo, step
            ).astype(F32)
    pending.append(copy(g_w_up, g_w_up_h))
    wait_all(loads[3])
    for lo in range(0, hidden, step):
        g_w_down[lo : lo + step, :] = take(width + hidden + lo, step).astype(F32)
    pending.append(copy(g_w_down, g_w_down_h))

    wait_all(loads[0])
    load_w.wait()
    first = pl.multiple_of(lax.axis_index("feat") * cols_mine, cols_mine)
    local = jnp.concatenate(
        [early[pl.ds(side * size + rest + first, cols_mine), :] for side in range(2)], axis=1
    )
    total = dot_nt(moment_s[pl.ds(first, cols_mine), :], w_qkv[...]) + local.astype(F32)
    column = lax.broadcasted_iota(jnp.int32, (cols_mine, 1), 0) + first
    g_w_enc[...] = jnp.where(column == columns - 1, 0.0, total)
    small = take(rest + columns, 16).astype(F32)
    last = moment_s[columns - 16 : columns, :]
    g_b_enc[...] = dot_nt(last, w_qkv[...])[15:16, :] + small[6:7, :]
    sums = last.astype(F32)[15:16, :]
    g_b_query[...] = sums[:, :width]
    g_b_value[...] = sums[:, 2 * width :]
    g_b_out[...] = small[6:7, :]
    g_gain_one[...] = small[4:5, :]
    g_shift_one[...] = small[5:6, :]
    g_b_up[...] = jnp.concatenate([small[3:4, :], small[11:12, :]], axis=1)
    g_b_down[...] = small[2:3, :]
    g_gain_two[...] = small[0:1, :]
    g_shift_two[...] = small[1:2, :]
    wait_all(pending)


def spec(kind):
    return pl.BlockSpec(memory_space={"v": pltpu.VMEM, "s": pltpu.SMEM, "h": pl.ANY}[kind])


def call(kernel, ins, args, outs, scratch, **params):
    return pl.pallas_call(
        kernel,
        out_shape=tuple(jax.ShapeDtypeStruct(shape, kind) for _, shape, kind in outs),
        in_specs=[spec(k) for k in ins],
        out_specs=tuple(spec(k) for k, _, _ in outs),
        scratch_shapes=[
            pltpu.SemaphoreType.DMA((entry,)) if isinstance(entry, int) else pltpu.VMEM(*entry)
            for entry in scratch
        ],
        compiler_params=pltpu.CompilerParams(vmem_limit_bytes=VMEM_BYTES, **params),
    )(*args)


def per_device(
    features, lengths, train_counts, used_features, w_enc, b_enc, w_qkv, b_query, b_value,
    w_out, b_out, gain_one, shift_one, w_up, b_up, w_down, b_down, gain_two, shift_two, cotangent,
):
    places = {"feat": lax.axis_size("feat"), "rows": lax.axis_size("rows")}
    feat_count = places["feat"]
    rows, cols_mine = features.shape
    columns = cols_mine * feat_count
    width = w_qkv.shape[0]
    hidden = w_up.shape[1]
    rows_mine = rows // feat_count
    half = width // 2
    early_group, late_group = 2, 4
    early_rows, early_parts, early_sems, early_land = reduce_plan(
        width + 2 * hidden + columns + 16, places, early_group
    )
    late_rows, late_parts, late_sems, late_land = reduce_plan(
        3 * columns // 2, places, late_group
    )
    stash_rows = max(
        rows_mine * (4 * width + 2 * hidden) // half, 2 * early_rows + 4 * PASSES * late_rows
    )
    row = lambda v: v.reshape(1, -1)
    gather_sems = 5 * (feat_count - 1)
    out, early, late, grad_x, w_enc_all = call(
        functools.partial(
            layer_kernel, places=places, early_parts=early_parts, early_group=early_group,
            late_parts=late_parts, late_group=late_group,
        ),
        "sss" + "v" * 12 + "h" * 5,
        (
            lengths, train_counts, used_features, features.T, w_enc, row(b_enc), row(b_query),
            row(b_value), row(b_out), row(gain_one), row(shift_one), row(b_up), row(b_down),
            row(gain_two), row(shift_two), w_qkv, w_out, w_up, w_down, cotangent,
        ),
        [
            ("h", (rows_mine, width), BF), ("h", (2 * early_rows, half), BF),
            ("h", (PASSES * 2 * late_rows, half), BF), ("v", (cols_mine, rows), F32),
            ("v", (columns, width), BF),
        ],
        [
            (w_out.shape, BF), (w_up.shape, BF), (w_down.shape, BF),
            ((rows_mine, width), BF),
            ((SLOTS, rows), BF), ((SLOTS, rows), BF), ((8, SLOTS), F32), ((rows, HD), BF),
            ((cols_mine, rows), F32), ((columns, rows), BF), ((2 * columns, 3 * width), BF),
            ((rows, width), BF), ((rows, width), BF), ((rows_mine, width), BF),
            ((rows_mine, width), F32), ((rows_mine, width), F32),
            ((HEADS, rows_mine, HD), BF), ((rows_mine, width), BF), ((HEADS, rows_mine, HD), BF),
            ((2, min(256, rows_mine), rows), F32),
            ((8, hidden), F32), ((stash_rows, half), BF), ((2 * early_rows, half), BF),
            ((early_rows, half), BF), ((early_land, half), BF),
            ((feat_count, cols_mine, rows), BF),
            ((PASSES, late_rows, half), BF), ((PASSES, late_land, half), BF),
            ((feat_count // 2, cols_mine, rows), BF), ((feat_count - 1, cols_mine, rows), BF),
            ((feat_count, cols_mine, rows_mine), BF), ((feat_count, cols_mine, rows_mine), BF),
            3 * (width // half) + 5 + 1 + PASSES, gather_sems, gather_sems, early_sems, early_sems,
            PASSES * late_sems, PASSES * late_sems,
            (feat_count - 1) * (rows // 512), (feat_count - 1) * (rows // 512), feat_count - 1,
            feat_count - 1,
        ],
        collective_id=0, has_side_effects=True,
    )
    vector = ("v", (1, width), F32)
    grads = call(
        finish_kernel,
        "hvvhvhh",
        (early, late, w_enc_all, w_qkv, row(b_enc), out, grad_x),
        [
            ("h", (rows_mine, width), BF), ("h", (cols_mine, rows), F32),
            ("v", (cols_mine, width), F32), vector,
            ("h", (width, 3 * width), F32), vector, vector, ("h", (width, width), F32), vector,
            vector, vector, ("h", (width, hidden), F32), ("v", (1, hidden), F32),
            ("h", (hidden, width), F32), vector, vector, vector,
        ],
        [
            ((2 * early_rows, half), BF), (w_qkv.shape, BF), ((width, 3 * width), F32),
            ((width, width), F32), ((width, hidden), F32), ((hidden, width), F32),
            ((columns, 3 * width), BF), ((rows_mine, width), BF), ((cols_mine, rows), F32), 20,
        ],
    )
    grads = [g.reshape(-1) if g.shape[0] == 1 else g for g in grads]
    return (grads[0], grads[1].T) + tuple(grads[2:])


def solution(mesh):
    whole = P()
    in_specs = (
        (P("rows", "feat"),) + (P("rows", None),) * 3 + (P("feat", None),) + (whole,) * 14
        + (P(("rows", "feat"), None),)
    )
    out_specs = (
        (P(("rows", "feat"), None), P("rows", "feat"), P("feat", None)) + (whole,) * 14
    )
    return jax.shard_map(
        per_device, mesh=mesh, in_specs=in_specs, out_specs=out_specs, check_vma=False
    )
```

```python
import functools
import math

import jax
import jax.numpy as jnp
from jax import lax
from jax.experimental import pallas as pl
from jax.experimental.pallas import tpu as pltpu
from jax.sharding import PartitionSpec as P

HEADS = 4
HD = 128
FEATS = 100
EPS = 1e-5
LOG2E = 1.4426950408889634
BIG = 1e30
SLOTS = 8
PASSES = 2
EARLY_AT = (0, 4, 7, 10)
LATE_AT = (1, 6)
VMEM_BYTES = 63 * 1024 * 1024

BF = jnp.bfloat16
F32 = jnp.float32
MESH = pl.DeviceIdType.MESH


def dot(a, b):
    return lax.dot_general(a, b, (((1,), (0,)), ((), ())), preferred_element_type=F32)


def dot_nt(a, b):
    return lax.dot_general(a, b, (((1,), (1,)), ((), ())), preferred_element_type=F32)


def dot_tn(a, b):
    return lax.dot_general(a, b, (((0,), (0,)), ((), ())), preferred_element_type=F32)


def split3(v):
    high = v.astype(BF)
    rest = v - high.astype(F32)
    mid = rest.astype(BF)
    return high, mid, (rest - mid.astype(F32)).astype(BF)


def dot_split(v, b):
    high, mid, small = split3(v)
    return dot(high, b) + dot(mid, b) + dot(small, b)


def aug_lanes(base, value):
    high, mid, small = (part.astype(F32) for part in split3(value))
    lane = lax.broadcasted_iota(jnp.int32, base.shape, 1)
    out = jnp.where(lane == SLOTS, high, base.astype(F32))
    out = jnp.where(lane == SLOTS + 1, mid, out)
    return jnp.where(lane == SLOTS + 2, small, out).astype(BF)

def bits_below(count):
    return [1 << i for i in range(count.bit_length() - 1)]


def bit_of(index, bit):
    return lax.rem(index // bit, 2)


def flip(index, bit):
    return index + bit * (1 - 2 * bit_of(index, bit))


def greet(peers):
    barrier = pltpu.get_barrier_semaphore()
    for peer in peers:
        pl.semaphore_signal(barrier, inc=1, device_id=peer, device_id_type=MESH)


def await_greetings(peers):
    pl.semaphore_wait(pltpu.get_barrier_semaphore(), len(peers))


def send(src, dst, sems, slot, peer):
    return pltpu.make_async_remote_copy(
        src_ref=src, dst_ref=dst, send_sem=sems[0].at[slot], recv_sem=sems[1].at[slot],
        device_id=peer, device_id_type=MESH,
    )


def gather_steps(feat_count):
    steps, held = [], [()]
    for bit in bits_below(feat_count)[::-1]:
        steps += [(path, bit) for path in held]
        held = held + [path + (bit,) for path in held]
    return steps


def feat_others(me, feat_count):
    bits = bits_below(feat_count)
    subsets = sorted(range(1, feat_count), key=lambda subset: bin(subset).count("1"))
    found = []
    for subset in subsets:
        at = me
        for bit in bits:
            if subset & bit:
                at = flip(at, bit)
        found.append(at)
    return found


class GatherFeat:
    def __init__(self, full, block, piece, sems, first, feat_count):
        self.full, self.block, self.piece = full, block, piece
        self.sems, self.first = sems, first
        self.steps = gather_steps(feat_count)
        self.me = lax.axis_index("feat")
        self.waited = set()

    def copy(self, number, at):
        path, bit = self.steps[number]
        index = self.me
        for done in path:
            index = flip(index, done)
        part = self.full.at[
            pl.ds(pl.multiple_of(index * self.block, self.block), self.block),
            pl.ds(at * self.piece, self.piece),
        ]
        slot = self.first + at * len(self.steps) + number
        return send(part, part, self.sems, slot, {"feat": flip(self.me, bit)})

    def arrived(self, number, at):
        if (number, at) not in self.waited:
            self.waited.add((number, at))
            self.copy(number, at).wait_recv()

    def start(self, at):
        for number, (path, _) in enumerate(self.steps):
            if not path:
                self.copy(number, at).start()

    def forward(self, at):
        for number, (path, _) in enumerate(self.steps):
            if path:
                self.arrived(self.steps.index((path[:-1], path[-1])), at)
                self.copy(number, at).start()

    def finish(self, at):
        for number in range(len(self.steps)):
            self.arrived(number, at)
        for number in range(len(self.steps)):
            self.copy(number, at).wait_send()


def chunked(items, size):
    return [items[i : i + size] for i in range(0, len(items), size)]


class AllReduce:
    def __init__(self, x, out, first_in, later_in, sems, places, parts, group, sem=0):
        self.x, self.out, self.sem, self.size = x, out, sem, sum(parts)
        self.first_in, self.later_in, self.sems = first_in, later_in, sems
        self.place = {axis: lax.axis_index(axis) for axis in places}
        self.core = bit_of(self.place["feat"], 1)
        groups = chunked(reduce_bits(places), group)
        self.depth = len(groups)
        self.parts = []
        self.count = sem + 2
        start = 0
        for number, size in enumerate(parts):
            turn = number * len(groups) // len(parts)
            at, landing, levels = start, start, []
            length = size
            for bits in groups[turn:] + groups[:turn]:
                length = length // 2 ** len(bits)
                member = sum(self.bit(b) << i for i, b in enumerate(bits))
                peers = []
                for subset in range(1, 2 ** len(bits)):
                    theirs = member
                    where = dict(self.place)
                    for i, (axis, bit) in enumerate(bits):
                        if subset >> i & 1:
                            theirs = theirs + (1 - 2 * self.bit((axis, bit))) * 2**i
                            where[axis] = flip(where[axis], bit)
                    peers.append((where, at + theirs * length, landing, self.count))
                    landing += length
                    self.count += 2
                at = at + member * length
                levels.append((peers, at, length))
            self.parts.append(levels)
            start += size

    def bit(self, which):
        return bit_of(self.place[which[0]], which[1])

    def rows(self, which, side, at, size):
        ref, base = which
        return ref.at[pl.ds(pl.multiple_of(base + side * self.size + at, 16), size)]

    def core_in(self):
        return send(
            self.rows(self.x, 1 - self.core, 0, self.size), self.first_in, self.sems, self.sem,
            self.peers()[0],
        )

    def core_out(self):
        half = self.rows(self.out, self.core, 0, self.size)
        return send(half, half, self.sems, self.sem + 1, self.peers()[0])

    def down(self, part, level):
        peers, _, size = self.parts[part][level]
        return [
            send(
                self.rows(self.x, self.core, at, size), self.later_in.at[pl.ds(landing, size)],
                self.sems, slot, where,
            )
            for where, at, landing, slot in peers
        ]

    def up(self, part, level):
        peers, at, size = self.parts[part][level]
        seg = self.rows(self.out, self.core, at, size)
        return [send(seg, seg, self.sems, slot + 1, where) for where, _, _, slot in peers]

    def stage(self, number):
        depth = self.depth
        everyone = range(len(self.parts))
        if number == 0:
            self.core_in().start()
        elif number == 1:
            self.core_in().wait()
            mine = self.rows(self.x, self.core, 0, self.size)
            mine[...] = (mine[...].astype(F32) + self.first_in[...].astype(F32)).astype(BF)
            for part in everyone:
                start_all(self.down(part, 0))
        elif number <= depth + 1:
            level = number - 2
            for part in everyone:
                wait_all(self.down(part, level))
                peers, at, size = self.parts[part][level]
                mine = self.rows(self.x, self.core, at, size)
                total = mine[...].astype(F32)
                for _, _, landing, _ in peers:
                    total = total + self.later_in[landing : landing + size, :].astype(F32)
                if level + 1 < depth:
                    mine[...] = total.astype(BF)
                    start_all(self.down(part, level + 1))
                else:
                    self.rows(self.out, self.core, at, size)[...] = total.astype(BF)
                    start_all(self.up(part, level))
        elif number <= 2 * depth + 1:
            level = depth - 1 - (number - depth - 2)
            for part in everyone:
                wait_all(self.up(part, level))
                if level > 0:
                    start_all(self.up(part, level - 1))
            if level == 0:
                self.core_out().start()
        else:
            self.core_out().wait()

    @property
    def stages(self):
        return 2 * self.depth + 3

    def peers(self):
        first = dict(self.place)
        first["feat"] = flip(first["feat"], 1)
        return [first] + [where for peers, _, _ in self.parts[0] for where, _, _, _ in peers]


def start_all(copies):
    for copy in copies:
        copy.start()


def wait_all(copies):
    for copy in copies:
        copy.wait()


def reduce_bits(places):
    return [("feat", b) for b in bits_below(places["feat"])[1:]] + [
        ("rows", b) for b in bits_below(places["rows"])
    ]


def reduce_plan(rows_needed, places, group):
    bits = reduce_bits(places)
    groups = chunked(bits, group)
    granule = 16 * 2 ** len(bits)
    units = -(-rows_needed // granule)
    first = -(-units * 2 // 3)
    parts = [first, units - first] if len(groups) > 1 and units > 1 else [units]
    parts = [size * granule for size in parts]
    sems = 2 + 2 * len(parts) * sum(2 ** len(g) - 1 for g in groups)
    landing = sum(parts)
    return sum(parts), parts, sems, landing


def tile_lanes(v, wide):
    return jnp.concatenate([v] * (wide // v.shape[1]), axis=1)


def table_masks(refs, mem_t, tr_t, tab):
    lengths, trains, used = refs
    tables = lengths.shape[1]
    slots, rows = mem_t.shape
    row = lax.broadcasted_iota(jnp.int32, (slots, rows), 0)
    at = lax.broadcasted_iota(jnp.int32, (slots, rows), 1)
    slot = lax.broadcasted_iota(jnp.int32, (8, slots), 1)
    line = lax.broadcasted_iota(jnp.int32, (8, slots), 0)
    member = jnp.zeros((slots, rows), jnp.bool_)
    train = jnp.zeros((slots, rows), jnp.bool_)
    counts = jnp.where(line < 2, 1, 0)
    start = jnp.int32(0)
    for j in range(tables):
        stop = start + lengths[0, j]
        learned = start + trains[0, j]
        here = (row == j) & (at >= start)
        member = member | (here & (at < stop))
        train = train | (here & (at < learned))
        counts = jnp.where((slot == j) & (line == 0), trains[0, j], counts)
        counts = jnp.where((slot == j) & (line > 0), used[0, j], counts)
        start = stop
    mem_t[...] = jnp.where(member, 1.0, 0.0).astype(BF)
    tr_t[...] = jnp.where(train, 1.0, 0.0).astype(BF)
    counts = counts.astype(F32)
    tab[...] = jnp.where(line == 1, jnp.sqrt(FEATS / jnp.maximum(counts, 1.0)), counts)


def key_masks(refs, key_aug):
    lengths, trains = refs
    lane = lax.broadcasted_iota(jnp.int32, (1, HD), 1)
    rows = key_aug.shape[0]
    low = jnp.full((1, HD), rows, jnp.int32)
    high = jnp.full((1, HD), 0, jnp.int32)
    start = jnp.int32(0)
    for j in range(lengths.shape[1]):
        low = jnp.where(lane == j, start, low)
        high = jnp.where(lane == j, start + trains[0, j], high)
        start = start + lengths[0, j]
    step = 512

    @pl.loop(0, rows // step)
    def _(block):
        token = lax.broadcasted_iota(jnp.int32, (step, HD), 0) + block * step
        wide = lax.broadcasted_iota(jnp.int32, (step, HD), 1)
        open_to = (token >= low) & (token < high)
        mask = jnp.where(wide < SLOTS, jnp.where(open_to, 0.0, -BIG), 0.0)
        ones = (wide >= SLOTS) & (wide < SLOTS + 3)
        key_aug[pl.ds(pl.multiple_of(block * step, step), step), :] = jnp.where(
            ones, 1.0, mask
        ).astype(BF)


def layer_kernel(
    lengths, trains, used, features_t, w_mine, b_enc, b_query, b_value, b_out, gain_one, shift_one,
    b_up, b_down, gain_two, shift_two,
    w_qkv_h, w_out_h, w_up_h, w_down_h, cot_h,
    out_h, early_h, late_h, grad_x, w_enc,
    w_out, w_up, w_down, cot,
    mem_t, tr_t, tab, key_aug, cent, normed_t, w_pair, keys, vals, query, enc, att,
    query_aug, grad_att, att_aug, sbuf,
    small, stash, early_x, first_e, later_e, grad_low,
    first_l, later_l, held, grad_in, own_low, own_in,
    local_sem, gsend, grecv, esend, erecv, lsend, lrecv, rsend, rrecv, osend, orecv,
    *, places, early_parts, early_group, late_parts, late_group,
):
    feat_count = places["feat"]
    me = lax.axis_index("feat")
    cols_mine, rows = features_t.shape
    columns, width = w_enc.shape
    hidden = w_up.shape[1]
    rows_mine = query.shape[0]
    row_lo = pl.multiple_of(me * rows_mine, rows_mine)
    col_lo = pl.multiple_of(me * cols_mine, cols_mine)
    half = width // 2

    taken = [0]

    def blocks(count):
        taken[0] += count
        return [
            stash.at[pl.ds(i * rows_mine, rows_mine)] for i in range(taken[0] - count, taken[0])
        ]

    wide_blocks, deep_blocks = width // half, hidden // half
    attl_s, gbl_s, o1_s, gffn_s = (blocks(wide_blocks) for _ in range(4))
    gpre_s, act_s = (blocks(deep_blocks) for _ in range(2))

    def fill(parts, at, value):
        for i, part in enumerate(parts):
            part[at, :] = value[:, i * half : (i + 1) * half]

    def read(parts):
        return jnp.concatenate([part[...] for part in parts], axis=1)

    early_size, late_size = sum(early_parts), sum(late_parts)
    late_x = [2 * early_size + turn * 4 * late_size for turn in range(PASSES)]
    late_o = [at + 2 * late_size for at in late_x]
    early = AllReduce(
        (early_x, 0), (stash, 0), first_e, later_e, (esend, erecv), places, early_parts, early_group
    )
    late_sems = lsend.shape[0] // PASSES
    lates = [
        AllReduce(
            (stash, late_x[turn]), (stash, late_o[turn]), first_l.at[turn], later_l.at[turn],
            (lsend, lrecv), places, late_parts, late_group, turn * late_sems,
        )
        for turn in range(PASSES)
    ]
    w_qkv = [
        [
            stash.at[pl.ds((part * wide_blocks + i) * width, width)]
            for i in range(wide_blocks)
        ]
        for part in range(3)
    ]
    loads = [
        pltpu.make_async_copy(src, dst, local_sem.at[i])
        for i, (src, dst) in enumerate(
            [
                (w_qkv_h.at[:, pl.ds(part * width + i * half, half)], block)
                for part, w_part in enumerate(w_qkv)
                for i, block in enumerate(w_part)
            ]
            + [(cot_h, cot), (w_out_h, w_out), (w_up_h, w_up), (w_down_h, w_down)]
        )
    ]
    start_all(loads)
    peers = lates[0].peers() + [{"feat": at} for at in feat_others(me, feat_count)[2:]]
    greet(peers)

    table_masks((lengths, trains, used), mem_t, tr_t, tab)
    step = 512
    pieces = [slice(at, at + step) for at in range(0, rows, step)]
    count = tab[0:1, :]
    mean = jnp.zeros((cols_mine, SLOTS), F32)
    for cut in pieces:
        mean = mean + dot_nt(features_t[:, cut], tr_t[:, cut])
    mean = mean / count
    var = jnp.zeros((cols_mine, SLOTS), F32)
    for cut in pieces:
        c = features_t[:, cut].astype(F32) - dot_split(mean, mem_t[:, cut])
        cent[:, cut] = c
        high, mid, _ = split3(c * c)
        var = var + (dot_nt(high, tr_t[:, cut]) + dot_nt(mid, tr_t[:, cut]))
    var = var / count
    column = (lax.broadcasted_iota(jnp.int32, (cols_mine, SLOTS), 0) + col_lo).astype(F32)
    is_last = (
        lax.broadcasted_iota(jnp.int32, (cols_mine, 1), 0) + col_lo == columns - 1
    )
    factor = jnp.where(
        column < tab[2:3, :], lax.rsqrt(jnp.maximum(var, 0.25)) * tab[1:2, :], 0.0
    )
    w_enc[pl.ds(col_lo, cols_mine), :] = w_mine[...]
    await_greetings(peers)
    steps = len(gather_steps(feat_count))
    gather_w = GatherFeat(w_enc, cols_mine, width, (gsend, grecv), 0, feat_count)
    gather_w.start(0)
    splits = 4
    piece = rows // splits
    gather_x = GatherFeat(normed_t, cols_mine, piece, (gsend, grecv), steps, feat_count)
    for at in range(splits):
        for cut in pieces[at * piece // step : (at + 1) * piece // step]:
            normed_t[pl.ds(col_lo, cols_mine), cut] = jnp.where(
                is_last, 1.0, cent[:, cut] * dot_split(factor, mem_t[:, cut])
            ).astype(BF)
        gather_x.start(at)

    key_masks((lengths, trains), key_aug)
    gather_w.forward(0)
    gather_w.finish(0)
    last = lax.broadcasted_iota(jnp.int32, (columns, 1), 0) == columns - 1
    w_enc[...] = jnp.where(last, 0.0, w_enc[...].astype(F32)).astype(BF)
    wait_all(loads[: 3 * wide_blocks])
    for part, w_part in enumerate(w_qkv):
        lanes = slice(part * width, (part + 1) * width)
        w_now = read(w_part)
        bias = dot_split(jnp.broadcast_to(b_enc[...], (8, width)), w_now)[0:1, :]
        if part != 1:
            bias = bias + (b_query if part == 0 else b_value)[...]
        high, mid, _ = split3(jnp.where(last, bias, dot(w_enc[...], w_now)))
        w_pair[0:columns, lanes] = high
        w_pair[columns:, lanes] = mid

    def project(at):
        for lo in range(at * piece, (at + 1) * piece, step):
            n = normed_t[:, lo : lo + step].astype(F32).T.astype(BF)
            both = jnp.concatenate([n, n], axis=1)
            keys[lo : lo + step, :] = dot(both, w_pair[:, width : 2 * width]).astype(BF)
            vals[lo : lo + step, :] = dot(both, w_pair[:, 2 * width :]).astype(BF)

    gather_x.forward(0)
    for at in range(splits):
        if at + 1 < splits:
            gather_x.forward(at + 1)
        gather_x.finish(at)
        project(at)
    block = min(256, rows_mine)
    scale = LOG2E / math.sqrt(HD)
    for lo in range(0, rows_mine, block):
        cols = pl.ds(pl.multiple_of(row_lo + lo, block), block)
        n = normed_t[:, cols].astype(F32).T.astype(BF)
        both = jnp.concatenate([n, n], axis=1)
        query[lo : lo + block, :] = (dot(both, w_pair[:, 0:width]) * scale).astype(BF)
        enc[lo : lo + block, :] = dot(n, w_enc[...]) + b_enc[...]

    q_step = min(256, rows_mine)
    k_step = 512
    ones = jnp.ones((k_step, HD), BF)

    @pl.loop(0, rows_mine // q_step)
    def _(number):
        lo = pl.multiple_of(number * q_step, q_step)
        q_rows = pl.ds(lo, q_step)
        cols = pl.ds(pl.multiple_of(row_lo + lo, q_step), q_step)
        table = jnp.concatenate(
            [mem_t[:, cols].astype(F32), jnp.zeros((HD - SLOTS, q_step), F32)], axis=0
        ).T.astype(BF)
        for head in range(HEADS):
            lanes = slice(head * HD, (head + 1) * HD)
            q = jnp.concatenate([query[q_rows, lanes], table], axis=1)
            peak = jnp.full((q_step, HD), -3e38, F32)
            for at in range(0, rows, k_step):
                k_rows = slice(at, at + k_step)
                k = jnp.concatenate([keys[k_rows, lanes], key_aug[k_rows, :]], axis=1)
                s = dot_nt(q, k)
                sbuf[head % 2, :, k_rows] = s
                for lo in range(0, k_step, HD):
                    peak = jnp.maximum(peak, s[:, lo : lo + HD])
            top = jnp.broadcast_to(jnp.max(peak, axis=1, keepdims=True), (q_step, HD))
            total = jnp.zeros((q_step, 2 * HD), F32)
            for at in range(0, rows, k_step):
                k_rows = slice(at, at + k_step)
                p = jnp.exp2(sbuf[head % 2, :, k_rows] - tile_lanes(top, k_step)).astype(BF)
                v = jnp.concatenate([vals[k_rows, lanes], ones], axis=1)
                total = total + dot(p, v)
            norm = total[:, HD:]
            att[q_rows, lanes] = total[:, :HD] / norm
            query_aug[head, q_rows, :] = aug_lanes(table, -(top + jnp.log2(norm)))

    wait_all(loads[3 * wide_blocks :])
    small[...] = jnp.zeros(small.shape, F32)

    def add_small(slot, value, wide):
        small[slot : slot + 1, 0:wide] += jnp.sum(value, axis=0, keepdims=True)

    def mean_of(v):
        return jnp.mean(v, axis=1, keepdims=True)

    for lo in range(0, rows_mine, block):
        at = slice(lo, lo + block)
        attended = att[at, :]
        attl = attended.astype(BF)
        fill(attl_s, at, attl)
        resid = enc[at, :] + dot(attl, w_out[...]) + b_out[...]
        ctr = resid - mean_of(resid)
        rstd1 = lax.rsqrt(mean_of(ctr * ctr) + EPS)
        n1 = ctr * rstd1
        o1 = n1 * gain_one[...] + shift_one[...]
        o1l = o1.astype(BF)
        fill(o1_s, at, o1l)
        pre = dot(o1l, w_up[...]) + b_up[...]
        cdf = 0.5 + 0.5 * lax.erf(pre * (1.0 / math.sqrt(2.0)))
        slope = cdf + pre * (jnp.exp(-0.5 * pre * pre) * (1.0 / math.sqrt(2.0 * math.pi)))
        actl = (pre * cdf).astype(BF)
        fill(act_s, at, actl)
        r2 = o1 + dot(actl, w_down[...]) + b_down[...]
        ctr2 = r2 - mean_of(r2)
        rstd2 = lax.rsqrt(mean_of(ctr2 * ctr2) + EPS)
        n2 = ctr2 * rstd2
        go = cot[at, :].astype(F32)
        cot[at, :] = (n2 * gain_two[...] + shift_two[...]).astype(BF)
        add_small(0, go * n2, width)
        add_small(1, go, width)
        dn = go * gain_two[...]
        g2 = rstd2 * (dn - mean_of(dn) - n2 * mean_of(dn * n2))
        gfl = g2.astype(BF)
        fill(gffn_s, at, gfl)
        add_small(2, g2, width)
        gpl = (dot_nt(gfl, w_down[...]) * slope).astype(BF)
        fill(gpre_s, at, gpl)
        add_small(3, gpl.astype(F32), hidden)
        g1 = dot_nt(gpl, w_up[...]) + g2
        add_small(4, g1 * n1, width)
        add_small(5, g1, width)
        dn1 = g1 * gain_one[...]
        gr = rstd1 * (dn1 - mean_of(dn1) - n1 * mean_of(dn1 * n1))
        add_small(6, gr, width)
        gbl = gr.astype(BF)
        fill(gbl_s, at, gbl)
        ga = dot_nt(gbl, w_out[...]).astype(BF)
        grad_att[at, :] = ga
        prod = ga.astype(F32) * attended
        zero = jnp.zeros((block, HD), BF)
        for head in range(HEADS):
            lanes = slice(head * HD, (head + 1) * HD)
            row_sum = jnp.sum(prod[:, lanes], axis=1, keepdims=True)
            att_aug[head, at, :] = aug_lanes(zero, jnp.broadcast_to(-row_sum, (block, HD)))

    store_out = pltpu.make_async_copy(cot, out_h, local_sem.at[3 * wide_blocks + 4])
    store_out.start()

    def pack(at, value):
        count = value.shape[0]
        early_x[at : at + count, :] = value[:, :half].astype(BF)
        early_x[early_size + at : early_size + at + count, :] = value[:, half:].astype(BF)

    own = pl.ds(row_lo, rows_mine)
    for i, part in enumerate(attl_s):
        pack(i * half, dot_tn(part[...], read(gbl_s)))
    base = width
    for i, part in enumerate(o1_s):
        up = dot_tn(part[...], read(gpre_s))
        for j in range(hidden // width):
            pack(base + j * width + i * half, up[:, j * width : (j + 1) * width])
    base = base + hidden
    for i, part in enumerate(act_s):
        pack(base + i * half, dot_tn(part[...], read(gffn_s)))
    base = base + hidden
    pack(base, dot(normed_t[:, own], read(gbl_s)))
    base = base + columns
    pack(base, jnp.concatenate([small[:, :width], small[:, width:]], axis=0))
    base = base + 16
    if base < early_size:
        pack(base, jnp.zeros((early_size - base, width), F32))
    early.stage(0)

    wide = HEADS // PASSES * HD
    grad_normed = sbuf.at[0, 0:columns, :]
    moment = sbuf.at[0, columns : 2 * columns, 0 : 3 * wide]
    mine = sbuf.at[1, 0:cols_mine, :]
    grad_own = sbuf.at[1, cols_mine : cols_mine + columns, 0:rows_mine]
    w_low = w_pair.at[0:columns, :]
    grad_own[...] = dot_nt(w_enc[...], read(gbl_s))
    chunks = rows // k_step
    plan = {}

    def place(when, stage):
        plan.setdefault(min(when, chunks * PASSES), []).append(stage)

    for number in range(1, early.stages):
        when = EARLY_AT[number - 1] if number <= len(EARLY_AT) else 16
        place(when * chunks * PASSES // 16, functools.partial(early.stage, number))
    for turn in range(PASSES - 1):
        for number in range(1, lates[turn].stages):
            when = LATE_AT[number - 1] if number <= len(LATE_AT) else 16
            place((turn + 1) * chunks + when * chunks // 8,
                  functools.partial(lates[turn].stage, number))

    order = bits_below(feat_count)
    index = {}
    for bit in order:
        for i in range(feat_count // (2 * bit)):
            index[bit, i] = len(index)

    def piece_at(number):
        return pl.ds(pl.multiple_of(number * k_step, k_step), k_step)

    def copy(bit, i, number):
        j = 1 - bit_of(me, bit) + 2 * i
        src = grad_low if bit == 1 else held
        at = j if bit == 1 else index[bit // 2, 0] + j
        return send(
            src.at[at, :, piece_at(number)], grad_in.at[index[bit, i], :, piece_at(number)],
            (rsend, rrecv), index[bit, i] * chunks + number, {"feat": flip(me, bit)},
        )

    def sum_start(level, number):
        bit = order[level]
        start_all([copy(bit, i, number) for i in range(feat_count // (2 * bit))])

    def sum_step(level, number):
        bit = order[level]
        cut = piece_at(number)
        for i in range(feat_count // (2 * bit)):
            copy(bit, i, number).wait()
            j = bit_of(me, bit) + 2 * i
            here = grad_low[j, :, cut] if bit == 1 else held[index[bit // 2, 0] + j, :, cut]
            total = here.astype(F32) + grad_in[index[bit, i], :, cut].astype(F32)
            if level + 1 < len(order):
                held[index[bit, i], :, cut] = total.astype(BF)
            else:
                mine[:, cut] = total
        if level + 1 < len(order):
            sum_start(level + 1, number)

    for turn in range(PASSES):
        heads = range(turn * HEADS // PASSES, (turn + 1) * HEADS // PASSES)
        at_pass = slice(turn * wide, (turn + 1) * wide)
        dq = att.at[:, at_pass]
        dq[...] = jnp.zeros((rows_mine, wide), F32)
        moment[...] = jnp.zeros(moment.shape, F32)
        w_kv = jnp.concatenate(
            [w_low[:, part * width + turn * wide : part * width + (turn + 1) * wide]
             for part in (1, 2)],
            axis=1,
        )

        @pl.loop(0, chunks)
        def _(number, turn=turn, heads=heads, dq=dq, w_kv=w_kv):
            k_rows = piece_at(number)
            aug = key_aug[k_rows, :]
            dks, dvs = [], []
            for head in heads:
                lanes = slice(head * HD, (head + 1) * HD)
                q = query[:, lanes]
                k = keys[k_rows, lanes]
                do = grad_att[:, lanes]
                s = dot_nt(
                    jnp.concatenate([k, aug], axis=1),
                    jnp.concatenate([q, query_aug[head]], axis=1),
                )
                p = jnp.exp2(s)
                dp = dot_nt(
                    jnp.concatenate([vals[k_rows, lanes], aug], axis=1),
                    jnp.concatenate([do, att_aug[head]], axis=1),
                )
                ds = (p * dp).astype(BF)
                dvs.append(dot(p.astype(BF), do).astype(BF))
                dks.append((dot(ds, q) * (1.0 / LOG2E)).astype(BF))
                into = slice((head - heads[0]) * HD, (head - heads[0] + 1) * HD)
                dq[:, into] += dot_tn(ds, k)
            grads = jnp.concatenate(dks + dvs, axis=1)
            moment[:, wide:] += dot(normed_t[:, k_rows], grads)
            product = dot_nt(w_kv, grads)
            if turn > 0:
                product = product + grad_normed[:, k_rows]
            if turn + 1 < PASSES:
                grad_normed[:, k_rows] = product
            else:
                for i in range(feat_count):
                    grad_low[i, :, k_rows] = product[i * cols_mine : (i + 1) * cols_mine, :].astype(
                        BF
                    )
                sum_start(0, number)

                @pl.when(number > 0)
                def _():
                    sum_step(0, number - 1)

            for when, stages in plan.items():
                if turn * chunks <= when < (turn + 1) * chunks:

                    @pl.when(number == when - turn * chunks)
                    def _(stages=stages):
                        for stage in stages:
                            stage()

        dql = (dq[...] * (1.0 / math.sqrt(HD))).astype(BF)
        moment[:, 0:wide] = dot(normed_t[:, own], dql)
        parts = jnp.concatenate(
            [moment[:, part * wide : (part + 1) * wide].astype(BF) for part in range(3)], axis=0
        )
        both = parts.shape[0] // 2
        for side in range(2):
            at = late_x[turn] + side * late_size
            stash[at : at + both, :] = parts[side * both : (side + 1) * both, :]
            if both < late_size:
                stash[at + both : at + late_size, :] = jnp.zeros((late_size - both, half), BF)
        lates[turn].stage(0)
        grad_own[...] += dot_nt(w_low[:, at_pass], dql)

    for i in range(feat_count):
        own_low[i] = grad_own[i * cols_mine : (i + 1) * cols_mine, :].astype(BF)
    swaps = []
    for number, other in enumerate(feat_others(me, feat_count)):
        swaps.append(
            send(own_low.at[other], own_in.at[me], (osend, orecv), number, {"feat": other})
        )
    start_all(swaps)
    own_in[me] = own_low[me]
    left = plan.get(chunks * PASSES, [])
    late = lates[-1]
    late.stage(1)
    sum_step(0, chunks - 1)
    for stage in left[:1]:
        stage()
    for level in range(1, len(order)):
        for number in range(chunks):
            sum_step(level, number)
    late.stage(2)
    wait_all(swaps)
    for i in range(feat_count):
        span = slice(i * rows_mine, (i + 1) * rows_mine)
        mine[:, span] += own_in[i].astype(F32)

    def gather(v, member):
        high, mid, _ = split3(v)
        return dot_nt(high, member) + dot_nt(mid, member)

    def expand(v, member):
        high, mid, _ = split3(v)
        return dot(high, member) + dot(mid, member)

    d_factor = jnp.zeros((cols_mine, SLOTS), F32)
    for cut in pieces:
        d_factor = d_factor + gather(mine[:, cut] * cent[:, cut], mem_t[:, cut])
    side = jnp.where(var > 0.25, 1.0, jnp.where(var == 0.25, 0.5, 0.0))
    d_var = d_factor * (-0.5) * factor / jnp.maximum(var, 0.25) * side
    pull = 2.0 * d_var / count
    d_mean = jnp.zeros((cols_mine, SLOTS), F32)
    for cut in pieces:
        dc = mine[:, cut] * expand(factor, mem_t[:, cut]) + cent[:, cut] * expand(
            pull, tr_t[:, cut]
        )
        grad_x[:, cut] = dc
        d_mean = d_mean - gather(dc, mem_t[:, cut])
    d_mean = d_mean / count
    for cut in pieces:
        grad_x[:, cut] = grad_x[:, cut] + expand(d_mean, tr_t[:, cut])
    for number in range(3, late.stages - 1):
        late.stage(number)
    for stage in left[1:]:
        stage()
    stores = [
        pltpu.make_async_copy(
            stash.at[pl.ds(at, count)], into, local_sem.at[3 * wide_blocks + 5 + i]
        )
        for i, (at, count, into) in enumerate(
            [(0, 2 * early_size, early_h)]
            + [
                (late_o[turn], 2 * late_size, late_h.at[pl.ds(turn * 2 * late_size, 2 * late_size)])
                for turn in range(PASSES)
            ]
        )
    ]
    start_all(stores[:-1])
    late.stage(late.stages - 1)
    stores[-1].start()
    store_out.wait()
    wait_all(stores)


def finish_kernel(
    early_h, late, w_enc, w_qkv_h, b_enc, out_in, grad_x_in,
    out, grad_x, g_w_enc, g_b_enc, g_w_qkv_h, g_b_query, g_b_value, g_w_out_h, g_b_out,
    g_gain_one, g_shift_one, g_w_up_h, g_b_up, g_w_down_h, g_b_down, g_gain_two, g_shift_two,
    early, w_qkv, g_w_qkv, g_w_out, g_w_up, g_w_down, moment_s, out_s, grad_x_s, sem,
):
    columns, width = w_enc.shape
    hidden = g_w_up.shape[1]
    cols_mine = g_w_enc.shape[0]
    places = [0]

    def copy(src, dst):
        places[0] += 1
        made = pltpu.make_async_copy(src, dst, sem.at[places[0] - 1])
        made.start()
        return made

    rest = width + 2 * hidden
    size = early.shape[0] // 2
    cuts = [
        pl.ds(rest, size - rest), pl.ds(0, width), pl.ds(width, hidden),
        pl.ds(width + hidden, hidden),
    ]
    loads = [
        [
            copy(
                early_h.at[pl.ds(side * size + cut.start, cut.size)],
                early.at[pl.ds(side * size + cut.start, cut.size)],
            )
            for side in range(2)
        ]
        for cut in cuts
    ]
    load_w = copy(w_qkv_h, w_qkv)
    passing = [copy(out_in, out_s), copy(grad_x_in, grad_x_s)]
    pending = []

    late_size = late.shape[0] // (2 * PASSES)
    wide = width // PASSES
    for turn in range(PASSES):
        starts = [(2 * turn + side) * late_size for side in range(2)]
        rows = jnp.concatenate([late[at : at + 3 * columns // 2, :] for at in starts], axis=0)
        for part in range(3):
            lo = part * width + turn * wide
            moment_s[:, lo : lo + wide] = rows[part * columns : (part + 1) * columns, :]
    bias = split3(b_enc[...])
    for lo in range(0, 3 * width, width):
        cut = slice(lo, lo + width)
        sums = moment_s[columns - 1 : columns, cut]
        outer = dot_tn(bias[0], sums) + dot_tn(bias[1], sums) + dot_tn(bias[2], sums)
        g_w_qkv[:, cut] = dot_tn(w_enc[...], moment_s[:, cut]) + outer
        lanes = pl.ds(lo, width)
        pending.append(copy(g_w_qkv.at[:, lanes], g_w_qkv_h.at[:, lanes]))

    wait_all(passing)
    pending += [copy(out_s, out), copy(grad_x_s, grad_x)]

    def take(lo, count):
        return jnp.concatenate(
            [early[lo : lo + count, :], early[size + lo : size + lo + count, :]], axis=1
        )

    step = 256
    wait_all(loads[1])
    for lo in range(0, width, step):
        g_w_out[lo : lo + step, :] = take(lo, step).astype(F32)
    pending.append(copy(g_w_out, g_w_out_h))
    wait_all(loads[2])
    for part in range(hidden // width):
        for lo in range(0, width, step):
            g_w_up[lo : lo + step, part * width : (part + 1) * width] = take(
                width + part * width + lo, step
            ).astype(F32)
    pending.append(copy(g_w_up, g_w_up_h))
    wait_all(loads[3])
    for lo in range(0, hidden, step):
        g_w_down[lo : lo + step, :] = take(width + hidden + lo, step).astype(F32)
    pending.append(copy(g_w_down, g_w_down_h))

    wait_all(loads[0])
    load_w.wait()
    first = pl.multiple_of(lax.axis_index("feat") * cols_mine, cols_mine)
    local = jnp.concatenate(
        [early[pl.ds(side * size + rest + first, cols_mine), :] for side in range(2)], axis=1
    )
    total = dot_nt(moment_s[pl.ds(first, cols_mine), :], w_qkv[...]) + local.astype(F32)
    column = lax.broadcasted_iota(jnp.int32, (cols_mine, 1), 0) + first
    g_w_enc[...] = jnp.where(column == columns - 1, 0.0, total)
    small = take(rest + columns, 16).astype(F32)
    last = moment_s[columns - 16 : columns, :]
    g_b_enc[...] = dot_nt(last, w_qkv[...])[15:16, :] + small[6:7, :]
    sums = last.astype(F32)[15:16, :]
    g_b_query[...] = sums[:, :width]
    g_b_value[...] = sums[:, 2 * width :]
    g_b_out[...] = small[6:7, :]
    g_gain_one[...] = small[4:5, :]
    g_shift_one[...] = small[5:6, :]
    g_b_up[...] = jnp.concatenate([small[3:4, :], small[11:12, :]], axis=1)
    g_b_down[...] = small[2:3, :]
    g_gain_two[...] = small[0:1, :]
    g_shift_two[...] = small[1:2, :]
    wait_all(pending)


def spec(kind):
    return pl.BlockSpec(memory_space={"v": pltpu.VMEM, "s": pltpu.SMEM, "h": pl.ANY}[kind])


def call(kernel, ins, args, outs, scratch, **params):
    return pl.pallas_call(
        kernel,
        out_shape=tuple(jax.ShapeDtypeStruct(shape, kind) for _, shape, kind in outs),
        in_specs=[spec(k) for k in ins],
        out_specs=tuple(spec(k) for k, _, _ in outs),
        scratch_shapes=[
            pltpu.SemaphoreType.DMA((entry,)) if isinstance(entry, int) else pltpu.VMEM(*entry)
            for entry in scratch
        ],
        compiler_params=pltpu.CompilerParams(vmem_limit_bytes=VMEM_BYTES, **params),
    )(*args)


def per_device(
    features, lengths, train_counts, used_features, w_enc, b_enc, w_qkv, b_query, b_value,
    w_out, b_out, gain_one, shift_one, w_up, b_up, w_down, b_down, gain_two, shift_two, cotangent,
):
    places = {"feat": lax.axis_size("feat"), "rows": lax.axis_size("rows")}
    feat_count = places["feat"]
    rows, cols_mine = features.shape
    columns = cols_mine * feat_count
    width = w_qkv.shape[0]
    hidden = w_up.shape[1]
    rows_mine = rows // feat_count
    half = width // 2
    early_group, late_group = 2, 4
    early_rows, early_parts, early_sems, early_land = reduce_plan(
        width + 2 * hidden + columns + 16, places, early_group
    )
    late_rows, late_parts, late_sems, late_land = reduce_plan(
        3 * columns // 2, places, late_group
    )
    stash_rows = max(
        rows_mine * (4 * width + 2 * hidden) // half, 2 * early_rows + 4 * PASSES * late_rows
    )
    row = lambda v: v.reshape(1, -1)
    gather_sems = 5 * (feat_count - 1)
    out, early, late, grad_x, w_enc_all = call(
        functools.partial(
            layer_kernel, places=places, early_parts=early_parts, early_group=early_group,
            late_parts=late_parts, late_group=late_group,
        ),
        "sss" + "v" * 12 + "h" * 5,
        (
            lengths, train_counts, used_features, features.T, w_enc, row(b_enc), row(b_query),
            row(b_value), row(b_out), row(gain_one), row(shift_one), row(b_up), row(b_down),
            row(gain_two), row(shift_two), w_qkv, w_out, w_up, w_down, cotangent,
        ),
        [
            ("h", (rows_mine, width), BF), ("h", (2 * early_rows, half), BF),
            ("h", (PASSES * 2 * late_rows, half), BF), ("v", (cols_mine, rows), F32),
            ("v", (columns, width), BF),
        ],
        [
            (w_out.shape, BF), (w_up.shape, BF), (w_down.shape, BF),
            ((rows_mine, width), BF),
            ((SLOTS, rows), BF), ((SLOTS, rows), BF), ((8, SLOTS), F32), ((rows, HD), BF),
            ((cols_mine, rows), F32), ((columns, rows), BF), ((2 * columns, 3 * width), BF),
            ((rows, width), BF), ((rows, width), BF), ((rows_mine, width), BF),
            ((rows_mine, width), F32), ((rows_mine, width), F32),
            ((HEADS, rows_mine, HD), BF), ((rows_mine, width), BF), ((HEADS, rows_mine, HD), BF),
            ((2, min(256, rows_mine), rows), F32),
            ((8, hidden), F32), ((stash_rows, half), BF), ((2 * early_rows, half), BF),
            ((early_rows, half), BF), ((early_land, half), BF),
            ((feat_count, cols_mine, rows), BF),
            ((PASSES, late_rows, half), BF), ((PASSES, late_land, half), BF),
            ((feat_count // 2, cols_mine, rows), BF), ((feat_count - 1, cols_mine, rows), BF),
            ((feat_count, cols_mine, rows_mine), BF), ((feat_count, cols_mine, rows_mine), BF),
            3 * (width // half) + 5 + 1 + PASSES, gather_sems, gather_sems, early_sems, early_sems,
            PASSES * late_sems, PASSES * late_sems,
            (feat_count - 1) * (rows // 512), (feat_count - 1) * (rows // 512), feat_count - 1,
            feat_count - 1,
        ],
        collective_id=0, has_side_effects=True,
    )
    vector = ("v", (1, width), F32)
    grads = call(
        finish_kernel,
        "hvvhvhh",
        (early, late, w_enc_all, w_qkv, row(b_enc), out, grad_x),
        [
            ("h", (rows_mine, width), BF), ("h", (cols_mine, rows), F32),
            ("v", (cols_mine, width), F32), vector,
            ("h", (width, 3 * width), F32), vector, vector, ("h", (width, width), F32), vector,
            vector, vector, ("h", (width, hidden), F32), ("v", (1, hidden), F32),
            ("h", (hidden, width), F32), vector, vector, vector,
        ],
        [
            ((2 * early_rows, half), BF), (w_qkv.shape, BF), ((width, 3 * width), F32),
            ((width, width), F32), ((width, hidden), F32), ((hidden, width), F32),
            ((columns, 3 * width), BF), ((rows_mine, width), BF), ((cols_mine, rows), F32), 20,
        ],
    )
    grads = [g.reshape(-1) if g.shape[0] == 1 else g for g in grads]
    return (grads[0], grads[1].T) + tuple(grads[2:])


def solution(mesh):
    whole = P()
    in_specs = (
        (P("rows", "feat"),) + (P("rows", None),) * 3 + (P("feat", None),) + (whole,) * 14
        + (P(("rows", "feat"), None),)
    )
    out_specs = (
        (P(("rows", "feat"), None), P("rows", "feat"), P("feat", None)) + (whole,) * 14
    )
    return jax.shard_map(
        per_device, mesh=mesh, in_specs=in_specs, out_specs=out_specs, check_vma=False
    )
```
